768 devices in a mesh: row: 12 (over z), col: 64 (over y, x, core).
Axes of the slice: x: 4, y: 8, z: 12, core: 2. Of those that a mesh axis runs over, the one named last changes fastest.
Arguments:
- obs_innovation: float32 [12, 64, 64, 32], P('row', 'col'), may hold values from -6 to 6
- obs_precision: float32 [12, 64, 64, 32], P('row', 'col'), may hold values from 0.5 to 4
- obs_offsets: float32 [12, 64, 64, 2, 32], P('row', 'col'), may hold values from 0 to 1
- obs_cell: int32 [12, 64, 64, 32], P('row', 'col'), may hold values from 0 to 130814, as said below
- obs_counts: int32 [12, 64, 64], P('row', 'col'), may hold values from 4 to 32, as said below
- land_sea: int32 [192, 16384], P('row', 'col'), may hold values 0 or 1
- diffusivity: float32 [192, 16384], P('row', 'col'), may hold values from 0.05 to 0.245
- background_std: bfloat16 [32, 192, 16384], P(None, 'row', 'col'), may hold values from 0.5 to 2
Outputs:
- increment: float32 [32, 192, 16384], P(None, 'row', 'col')
The draws below stay inside these ranges and needn't reach their ends.
Inputs may be any that keep to these rules, and one draw needn't show every extreme that they name: Live slots are the first obs_counts[r, s, d] of the 32 slots; in every tile row some destination tile column receives 32 records from every source tile column. `obs_cell`: encodes c * 16 * 256 + i * 256 + j with channel c < 32, i < 15, j < 255, so all four interpolation cells lie in the destination tile.
All inputs are finite; a program needn't handle non-finite values. No bound on the sum of `land_sea` on one device may be relied on, other than what follows from the above.
Results may differ from the reference program's by a relative error of at most 0.0012.
Values sent between devices are 32-bit elements; how exact they have to be, the bound alone decides.
No kernel may reach another device: no remote copies, remote signals or barrier semaphores. Data moves between devices by JAX's collectives and lax.ppermute only.
A program may use at most 32 MiB of HBM per device.

```python
import math
import jax
import jax.numpy as jnp
from jax import lax

NCH = 32
CY = 16
CX = 256
REC_CAP = 32
SWEEPS = 6
TILE_ROWS = 12
TILE_COLS = 64
NY = 192
NX = 16384


def draw_obs_counts(key, part):
    key_base, key_hot, key_force = jax.random.split(jax.random.fold_in(key, 11), 3)
    base_count = jax.random.randint(key_base, (TILE_ROWS, TILE_COLS, TILE_COLS), max(1, REC_CAP // 8), REC_CAP // 2 + 1)
    hot_dest = jax.random.randint(key_hot, (TILE_ROWS, 1, TILE_COLS), 0, 8) == 0
    forced = jax.random.randint(key_force, (TILE_ROWS, 1, 1), 0, TILE_COLS)
    dest_ids = lax.broadcasted_iota(jnp.int32, (TILE_ROWS, 1, TILE_COLS), 2)
    hot_dest = jnp.logical_or(hot_dest, dest_ids == forced)
    return jnp.where(hot_dest, REC_CAP, base_count).astype(jnp.int32)


def draw_obs_cell(key, part):
    key_chan, key_row, key_col = jax.random.split(jax.random.fold_in(key, 23), 3)
    shape_all = (TILE_ROWS, TILE_COLS, TILE_COLS, REC_CAP)
    channel = jax.random.randint(key_chan, shape_all, 0, NCH)
    cell_row = jax.random.randint(key_row, shape_all, 0, CY - 1)
    cell_col = jax.random.randint(key_col, shape_all, 0, CX - 1)
    encoded = channel * (CY * CX) + cell_row * CX + cell_col
    encoded = encoded.at[0, 0, 0, 0].set(NCH * CY * CX - CX - 2)
    encoded = encoded.at[0, 0, 0, 1].set(0)
    return encoded.astype(jnp.int32)


def place_ends(drawn, own_key, low, high):
    place = [jax.random.randint(jax.random.fold_in(own_key, axis), (), 0, length) for axis, length in enumerate(drawn.shape)]
    widest = drawn.shape.index(max(drawn.shape))
    neighbour = place[:widest] + [(place[widest] + 1) % drawn.shape[widest]] + place[widest + 1:]
    return drawn.at[tuple(place)].set(low).at[tuple(neighbour)].set(high)


def block_levels(stream_key, dims, cuts, least, largest):
    loudness = 1.0
    for position, blocks in cuts:
        heights = jax.random.uniform(jax.random.fold_in(jax.random.fold_in(stream_key, 6), position), (blocks,), jnp.float32, least / len(cuts), largest / len(cuts))
        loudness = loudness * jnp.repeat(jnp.exp(heights), dims[position] // blocks).reshape((-1,) + (1,) * (len(dims) - 1 - position))
    return loudness


def scatter_about(own_key, shape, scale, most, cuts=(), kind=jnp.bfloat16):
    drawn = jax.random.normal(own_key, shape, jnp.float32) * scale
    if len(cuts) > 0:
        drawn = block_levels(own_key, shape, cuts, -0.22, 0.18) * drawn
    return jnp.clip(drawn, min=-most, max=most).astype(kind)


def setup_inputs(seed: int = 0) -> dict:
    streams_of = jax.random.split(jax.random.key(seed), 9)
    return {
        "obs_innovation": scatter_about(streams_of[0], (TILE_ROWS, TILE_COLS, TILE_COLS, REC_CAP), 1.0, 6.0, ((0, 12), (1, 64)), jnp.float32),
        "obs_precision": jnp.clip(jnp.exp(math.log(4.0) - 2.0794415 * jax.random.uniform(streams_of[1], (TILE_ROWS, TILE_COLS, TILE_COLS, REC_CAP), jnp.float32) ** block_levels(streams_of[1], (TILE_ROWS, TILE_COLS, TILE_COLS, REC_CAP), ((0, 12), (1, 64)), -0.2, 0.2)), 0.5, 4.0),
        "obs_offsets": jnp.clip(1.0 * jax.random.uniform(streams_of[2], (TILE_ROWS, TILE_COLS, TILE_COLS, 2, REC_CAP), jnp.float32) ** block_levels(streams_of[2], (TILE_ROWS, TILE_COLS, TILE_COLS, 2, REC_CAP), ((0, 12), (1, 64)), -0.2, 0.2), 0.0, 1.0),
        "obs_cell": draw_obs_cell(jax.random.fold_in(streams_of[8], 71), 0),
        "obs_counts": draw_obs_counts(jax.random.fold_in(streams_of[8], 71), 0),
        "land_sea": place_ends((jax.random.randint(streams_of[5], (NY, NX), 0, 4) < 3).astype(jnp.int32), jax.random.fold_in(streams_of[5], 1), 0, 1),
        "diffusivity": jnp.clip(jnp.exp(math.log(0.245) - 1.5892352 * jax.random.uniform(streams_of[6], (NY, NX), jnp.float32) ** block_levels(streams_of[6], (NY, NX), ((0, 12), (1, 64)), -0.2, 0.2)), 0.05, 0.245),
        "background_std": jnp.clip(jnp.exp(math.log(2.0) - 1.3862944 * jax.random.uniform(streams_of[7], (NCH, NY, NX), jnp.float32) ** block_levels(streams_of[7], (NCH, NY, NX), ((1, 12), (2, 64)), -0.2, 0.2)), 0.5, 2.0).astype(jnp.bfloat16),
    }


def corner_terms(weighted, east_frac, north_frac):
    return jnp.stack([(1.0 - east_frac) * (1.0 - north_frac) * weighted, east_frac * (1.0 - north_frac) * weighted, (1.0 - east_frac) * north_frac * weighted, east_frac * north_frac * weighted], axis=-2)

def reference(obs_innovation, obs_precision, obs_offsets, obs_cell, obs_counts, land_sea, diffusivity, background_std):
    total_rows = TILE_ROWS * CY
    total_cols = TILE_COLS * CX
    slot_ids = lax.broadcasted_iota(jnp.int32, obs_innovation.shape, 3)
    live_slot = slot_ids < obs_counts[..., None]
    weighted = jnp.where(live_slot, obs_innovation * obs_precision, jnp.float32(0.0))
    corners = corner_terms(weighted, obs_offsets[:, :, :, 0, :], obs_offsets[:, :, :, 1, :])
    channel = obs_cell // (CY * CX)
    within = obs_cell % (CY * CX)
    cell_row = within // CX
    cell_col = within % CX
    tile_row = lax.broadcasted_iota(jnp.int32, obs_cell.shape, 0)
    tile_col = lax.broadcasted_iota(jnp.int32, obs_cell.shape, 2)
    flat_cell = (tile_row * CY + cell_row) * total_cols + tile_col * CX + cell_col
    steps_off = jnp.array([0, 1, total_cols, total_cols + 1], dtype=jnp.int32)
    targets = flat_cell[..., None, :] + steps_off[:, None]
    channel_all = jnp.broadcast_to(channel[..., None, :], targets.shape)
    sea_mask = land_sea.astype(jnp.float32)
    diffusion = diffusivity * sea_mask
    diff_pad = jnp.pad(diffusion, ((1, 1), (0, 0)))
    east_face = jnp.sqrt(diffusion * jnp.roll(diffusion, -1, 1))
    west_face = jnp.sqrt(diffusion * jnp.roll(diffusion, 1, 1))
    north_face = jnp.sqrt(diffusion * diff_pad[2:])
    south_face = jnp.sqrt(diffusion * diff_pad[:-2])
    corner_flat = corners.reshape(-1)

    def one_channel(which):
        chosen = jnp.where(channel_all == which, targets, total_rows * total_cols).reshape(-1)
        adjoint = jnp.zeros((total_rows * total_cols,), jnp.float32).at[chosen].add(corner_flat, mode='drop')
        adjoint = adjoint.reshape(total_rows, total_cols)
        spread = background_std[which].astype(jnp.float32)
        state = spread * sea_mask * adjoint
        for sweep_index in range(SWEEPS):
            rowpad = jnp.pad(state, ((1, 1), (0, 0)))
            state = state + (east_face * (jnp.roll(state, -1, 1) - state) + west_face * (jnp.roll(state, 1, 1) - state) + (north_face * (rowpad[2:] - state) + south_face * (rowpad[:-2] - state)))
        return spread * sea_mask * state
    return lax.map(one_channel, jnp.arange(NCH, dtype=jnp.int32))
```

```python
import jax
import jax.numpy as jnp
from jax import lax
from jax.experimental import pallas as pl
from jax.experimental.pallas import tpu as pltpu
from jax.sharding import PartitionSpec as P

SWEEPS = 6
LANES = 128
RIM = 8
VMEM_BYTES = 24 * 1024 * 1024

WHOLE = pl.BlockSpec(memory_space=pltpu.VMEM)
NT = (((1,), (1,)), ((), ()))


def kernel_call(body, name, outs, inputs, scratch=(), flops=0, moved=0):
    return pl.pallas_call(
        body,
        name=name,
        out_shape=outs,
        in_specs=[WHOLE] * len(inputs),
        out_specs=jax.tree.map(lambda _: WHOLE, outs),
        scratch_shapes=list(scratch),
        compiler_params=pltpu.CompilerParams(vmem_limit_bytes=VMEM_BYTES),
        cost_estimate=pl.CostEstimate(flops=flops, bytes_accessed=moved, transcendentals=0),
    )(*inputs)


def f32(*shape):
    return jax.ShapeDtypeStruct(shape, jnp.float32)


def pack_body(innovation, precision, offsets, cells, counts, out, tile, rows):
    slots, dests = innovation.shape
    live = lax.broadcasted_iota(jnp.int32, (slots, dests), 0) < counts[...]
    tile[0:slots, 0:dests] = jnp.where(live, innovation[...] * precision[...], 0.0)
    tile[slots : 2 * slots, 0:dests] = offsets[0]
    tile[2 * slots : 3 * slots, 0:dests] = offsets[1]
    tile[3 * slots : 4 * slots, 0:dests] = cells[...].astype(jnp.float32)
    rows[...] = tile[...].T
    for d in range(dests):
        for k in range(3):
            out[d, :, k * LANES : (k + 1) * LANES] = rows[pl.ds((d + k - 1) % dests, 1), :]


def fixed_body(std, sea, diffusivity, spread, coef, first, last, stage):
    channels, rows, cols = std.shape
    mask = sea[...].astype(jnp.float32)
    product = std[...].astype(jnp.float32) * mask[None]
    for part in range(cols // LANES):
        stage[part] = product[:, :, part * LANES : (part + 1) * LANES].reshape(channels * rows, LANES)
    coef[...] = diffusivity[...] * mask
    lane = lax.broadcasted_iota(jnp.int32, (channels, LANES), 1)
    ends = [jnp.zeros((channels, LANES), jnp.float32)] * 2
    for i in range(rows):
        here = [stage[part, pl.ds(i, channels, stride=rows), :] for part in range(cols // LANES)]
        for part, values in enumerate(here):
            spread[i, :, part * LANES : (part + 1) * LANES] = values
        inside = (lane >= RIM * i) & (lane < RIM * (i + 1))
        ends[0] = jnp.where(inside, pltpu.roll(here[0], (RIM * i) % LANES, 1), ends[0])
        ends[1] = jnp.where(inside, pltpu.roll(here[-1], (RIM * i + RIM) % LANES, 1), ends[1])
    lane_row = lax.broadcasted_iota(jnp.int32, (1, LANES), 1)
    for which, rim in enumerate((first, last)):
        edge = coef[:, 0:LANES] if which == 0 else coef[:, cols - LANES : cols]
        packed = jnp.zeros((1, LANES), jnp.float32)
        for i in range(rows):
            inside = (lane_row >= RIM * i) & (lane_row < RIM * (i + 1))
            turned = pltpu.roll(edge[i : i + 1], (RIM * i + RIM * which) % LANES, 1)
            packed = jnp.where(inside, turned, packed)
        rim[0:channels] = ends[which]
        rim[channels : channels + 8] = jnp.broadcast_to(packed, (8, LANES))


def record_fields(block, slots):
    quarter = block.shape[0] // 4
    lane = lax.broadcasted_iota(jnp.int32, (quarter, LANES), 1)
    fields = []
    for f in range(4):
        joined = None
        for b in range(4):
            part = block[b * quarter : (b + 1) * quarter]
            turn = (slots * (b - f)) % LANES
            if turn:
                part = pltpu.roll(part, turn, 1)
            joined = part if b == 0 else jnp.where(lane >= slots * b, part, joined)
        fields.append(joined)
    return fields


def split(values):
    high = values.astype(jnp.bfloat16)
    low = (values - high.astype(jnp.float32)).astype(jnp.bfloat16)
    return high, low


def two_hot(size, position, at, after):
    row = lax.broadcasted_iota(jnp.int32, (size, position.shape[1]), 0) - position
    return jnp.where(row == 0, at, jnp.where(row == 1, after, 0.0))


def dot_split(a, b):
    dot = lambda x, y: lax.dot_general(x[...], y[...], NT, preferred_element_type=jnp.float32)
    return dot(a[0], b[0]) + (dot(a[0], b[1]) + dot(a[1], b[0]))


def build_body(
    arrived, spread, coef, rim_left, rim_right,
    state, coef_out, to_up, to_down,
    field_ref, a_high, a_low, b_high, b_low, c_high, c_low, d_high, d_low,
):
    rows, channels, cols = spread.shape
    slots = LANES // 4
    blocks = field_ref.shape[2]

    for k in range(3):
        for f, values in enumerate(record_fields(arrived[:, 0, k * LANES : (k + 1) * LANES], slots)):
            field_ref[k, f] = values

    def unpack(k, n):
        weight, east, north, cell = [field_ref[k, f, pl.ds(n, 1), :] for f in range(4)]
        cell = cell.astype(jnp.int32)
        return weight, east, north, cell >> 12, (cell >> 8) & 15, cell & 255

    def own(n, carry):
        weight, east, north, channel, i, j = unpack(1, n)
        here = pl.ds(pl.multiple_of(n * LANES, LANES), LANES)
        hot = lax.broadcasted_iota(jnp.int32, (channels, LANES), 0) == channel
        by_row = two_hot(rows, i, weight * (1.0 - north), weight * north)
        high = by_row.astype(jnp.bfloat16).astype(jnp.float32)
        low = by_row - high
        for row in range(rows):
            at = slice(row * channels, (row + 1) * channels)
            a_high[at, here] = jnp.where(hot, high[row : row + 1], 0.0).astype(jnp.bfloat16)
            a_low[at, here] = jnp.where(hot, low[row : row + 1], 0.0).astype(jnp.bfloat16)
        b_high[:, here], b_low[:, here] = split(two_hot(cols, j, 1.0 - east, east))
        return carry

    lax.fori_loop(0, blocks, own, 0)

    def rim(n, carry):
        here = pl.ds(pl.multiple_of(n * LANES, LANES), LANES)
        for side, (k, base) in enumerate(((0, cols - RIM), (2, 0))):
            weight, east, north, channel, i, j = unpack(k, n)
            hot = lax.broadcasted_iota(jnp.int32, (channels, LANES), 0) == channel
            c_high[side, :, here], c_low[side, :, here] = split(jnp.where(hot, weight, 0.0))
            by_row = two_hot(rows, i, 1.0 - north, north)
            by_col = two_hot(RIM, j - base, 1.0 - east, east)
            both = (by_row[:, None, :] * by_col[None, :, :]).reshape(rows * RIM, LANES)
            d_high[side, :, here], d_low[side, :, here] = split(both)
        return carry

    lax.fori_loop(0, blocks, rim, 0)

    adjoint = dot_split((a_high, a_low), (b_high, b_low))
    sides = []
    for side, halo in enumerate((rim_left, rim_right)):
        product = dot_split((c_high.at[side], c_low.at[side]), (d_high.at[side], d_low.at[side]))
        sides.append(product * halo[0:channels])

    lane = lax.broadcasted_iota(jnp.int32, (channels, LANES), 1)
    lane_row = lax.broadcasted_iota(jnp.int32, (1, LANES), 1)

    def outer(left, right, i, lanes):
        left = pltpu.roll(left, (LANES - RIM - RIM * i) % LANES, 1)
        right = pltpu.roll(right, (LANES - RIM * i) % LANES, 1)
        return jnp.where(lanes < RIM, right, jnp.where(lanes >= LANES - RIM, left, 0.0))

    coef_out[:, 0:cols] = coef[...]
    tails = []
    for i in range(rows):
        state[i, :, 0:cols] = adjoint[i * channels : (i + 1) * channels] * spread[i]
        tail = outer(sides[0], sides[1], i, lane)
        state[i, :, cols : cols + LANES] = tail
        tails.append(tail)
        coef_out[i : i + 1, cols : cols + LANES] = outer(
            rim_left[channels : channels + 1], rim_right[channels : channels + 1], i, lane_row
        )

    for out, start in ((to_down, 0), (to_up, rows - SWEEPS)):
        packed = jnp.zeros((channels, LANES), jnp.float32)
        for q in range(SWEEPS):
            i = start + q
            out[q * channels : (q + 1) * channels, :] = state[i, :, 0:cols]
            inside = (lane >= 2 * RIM * q) & (lane < 2 * RIM * (q + 1))
            packed = jnp.where(inside, pltpu.roll(tails[i], (2 * RIM * q + RIM) % LANES, 1), packed)
        base = SWEEPS * channels
        half = channels // 2
        out[base : base + half, 0:LANES] = packed[0:half]
        out[base : base + half, LANES : 2 * LANES] = packed[half:channels]
        base = base + half
        out[base : base + 8, :] = jnp.zeros((8, cols), jnp.float32)
        out[base : base + SWEEPS, :] = coef_out[start : start + SWEEPS, 0:cols]
        out[base + 8 : base + 16, :] = jnp.zeros((8, cols), jnp.float32)
        out[base + 8 : base + 8 + SWEEPS, 0:LANES] = coef_out[start : start + SWEEPS, cols : cols + LANES]


def sweep_body(state, coef, spread, from_down, from_up, out, work, east, north, stage):
    rows, channels, width = state.shape
    cols = width - LANES
    depth = rows + 2 * SWEEPS
    groups = channels // 8
    half = channels // 2
    lane = lax.broadcasted_iota(jnp.int32, (channels, LANES), 1)

    stage[...] = jnp.zeros_like(stage)
    stage[SWEEPS : SWEEPS + rows, :] = coef[...]
    for block, start in ((from_down, 0), (from_up, SWEEPS + rows)):
        base = SWEEPS * channels
        packed = jnp.concatenate([block[base : base + half, 0:LANES], block[base : base + half, LANES : 2 * LANES]], axis=0)
        for q in range(SWEEPS):
            work[start + q, :, 0:cols] = block[q * channels : (q + 1) * channels, :]
            tail = pltpu.roll(packed, (LANES - 2 * RIM * q - RIM) % LANES, 1)
            work[start + q, :, cols:width] = jnp.where((lane < RIM) | (lane >= LANES - RIM), tail, 0.0)
        base = base + half
        stage[start : start + SWEEPS, 0:cols] = block[base : base + SWEEPS, :]
        stage[start : start + SWEEPS, cols:width] = block[base + 8 : base + 8 + SWEEPS, 0:LANES]
    for i in range(rows):
        work[SWEEPS + i] = state[i]

    centre = stage[...]
    east_face = jnp.sqrt(centre * pltpu.roll(centre, width - 1, 1))
    north_face = jnp.sqrt(centre * pltpu.roll(centre, centre.shape[0] - 1, 0))
    for y in range(depth):
        east[y] = jnp.broadcast_to(east_face[y : y + 1], (8, width))
        north[y] = jnp.broadcast_to(north_face[y : y + 1], (8, width))

    def load(y):
        return [work[y, 8 * g : 8 * (g + 1), :] for g in range(groups)]

    for t in range(1, SWEEPS + 1):
        below, current = load(t - 1), load(t)
        flux = [north[t - 1] * (c - b) for b, c in zip(below, current)]

        def step(y, carry):
            now, flux_in = carry
            above = load(y + 1)
            e, n = east[y], north[y]
            flux_out = []
            for g in range(groups):
                s = now[g]
                along = e * (pltpu.roll(s, width - 1, 1) - s)
                across = n * (above[g] - s)
                flux_out.append(across)
                work[y, 8 * g : 8 * (g + 1), :] = s + ((along - pltpu.roll(along, 1, 1)) + (across - flux_in[g]))
            return above, flux_out

        lax.fori_loop(t, depth - t, step, (current, flux))

    for i in range(rows):
        result = work[SWEEPS + i, :, 0:cols] * spread[i]
        for part in range(cols // LANES):
            first = (i // 8) * 8 * (cols // LANES) + part * 8 + i % 8
            out[pl.ds(first, channels, stride=rows * cols // LANES), :] = result[:, part * LANES : (part + 1) * LANES]


def per_device(
    obs_innovation,
    obs_precision,
    obs_offsets,
    obs_cell,
    obs_counts,
    land_sea,
    diffusivity,
    background_std,
):
    dests, slots = obs_innovation.shape[2:]
    channels, rows, cols = background_std.shape
    width = cols + LANES
    count_rows, count_cols = lax.axis_size("row"), lax.axis_size("col")
    records = dests * slots

    by_slot = lambda x: x.reshape(dests, slots).T
    offsets = obs_offsets.reshape(dests, 2, slots).transpose(1, 2, 0)
    packed = kernel_call(
        pack_body,
        "pack_records",
        f32(dests, 1, 3 * LANES),
        (by_slot(obs_innovation), by_slot(obs_precision), offsets, by_slot(obs_cell), obs_counts.reshape(1, dests)),
        [pltpu.VMEM((LANES, LANES), jnp.float32)] * 2,
        moved=200_000,
    )
    arrived = lax.all_to_all(packed, "col", split_axis=0, concat_axis=0, tiled=True)

    spread, coef, first, last = kernel_call(
        fixed_body,
        "fixed_fields",
        (f32(rows, channels, cols), f32(rows, cols), f32(channels + 8, LANES), f32(channels + 8, LANES)),
        (background_std, land_sea, diffusivity),
        [pltpu.VMEM((cols // LANES, channels * rows, LANES), jnp.float32)],
        moved=2_000_000,
    )
    to_east = [(i, (i + 1) % count_cols) for i in range(count_cols)]
    to_west = [(j, i) for i, j in to_east]
    rim_left = lax.ppermute(last, "col", to_east)
    rim_right = lax.ppermute(first, "col", to_west)

    slab = SWEEPS * channels + channels // 2 + 16
    blocks = records // LANES
    bf16 = lambda *shape: pltpu.VMEM(shape, jnp.bfloat16)
    state, coef_wide, to_up, to_down = kernel_call(
        build_body,
        "build_state",
        (f32(rows, channels, width), f32(rows, width), f32(slab, cols), f32(slab, cols)),
        (arrived, spread, coef, rim_left, rim_right),
        [pltpu.VMEM((3, 4, blocks, LANES), jnp.float32)]
        + [bf16(rows * channels, records)] * 2
        + [bf16(cols, records)] * 2
        + [bf16(2, channels, records)] * 2
        + [bf16(2, rows * RIM, records)] * 2,
        moved=10_000_000,
    )
    up = [(i, i + 1) for i in range(count_rows - 1)]
    down = [(j, i) for i, j in up]
    from_down = lax.ppermute(to_up, "row", up)
    from_up = lax.ppermute(to_down, "row", down)

    depth = rows + 2 * SWEEPS
    out = kernel_call(
        sweep_body,
        "sweeps",
        f32(channels * rows * cols // LANES, LANES),
        (state, coef_wide, spread, from_down, from_up),
        [
            pltpu.VMEM((depth, channels, width), jnp.float32),
            pltpu.VMEM((depth, 8, width), jnp.float32),
            pltpu.VMEM((depth, 8, width), jnp.float32),
            pltpu.VMEM(((depth + 7) // 8 * 8, width), jnp.float32),
        ],
        moved=10_000_000,
    )
    out = out.reshape(channels, rows // 8, cols // LANES, 8, LANES)
    return out.transpose(0, 1, 3, 2, 4).reshape(channels, rows, cols)


def solution(mesh):
    placed = (
        P("row", "col", None, None),
        P("row", "col", None, None),
        P("row", "col", None, None, None),
        P("row", "col", None, None),
        P("row", "col", None),
        P("row", "col"),
        P("row", "col"),
        P(None, "row", "col"),
    )
    return jax.shard_map(
        per_device, mesh=mesh, in_specs=placed, out_specs=P(None, "row", "col"), check_vma=False
    )
```

```python
import jax
import jax.numpy as jnp
from jax import lax
from jax.experimental import pallas as pl
from jax.experimental.pallas import tpu as pltpu
from jax.sharding import PartitionSpec as P

SWEEPS = 6
LANES = 128
CHUNKS = 4
RIM = 8
VMEM_BYTES = 24 * 1024 * 1024
ALL_VMEM_BYTES = 58 * 1024 * 1024

WHOLE = pl.BlockSpec(memory_space=pltpu.VMEM)
NT = (((1,), (1,)), ((), ()))


def kernel_call(body, name, outs, inputs, scratch=(), moved=0, place=pltpu.VMEM, grant=VMEM_BYTES):
    return pl.pallas_call(
        body,
        name=name,
        out_shape=outs,
        in_specs=[pl.BlockSpec(memory_space=place)] * len(inputs),
        out_specs=jax.tree.map(lambda _: WHOLE, outs),
        scratch_shapes=list(scratch),
        compiler_params=pltpu.CompilerParams(vmem_limit_bytes=grant),
        cost_estimate=pl.CostEstimate(flops=0, bytes_accessed=moved, transcendentals=0),
    )(*inputs)


def f32(*shape):
    return jax.ShapeDtypeStruct(shape, jnp.float32)


def pack_body(innovation_in, precision_in, offsets_in, cells_in, counts_in, out, innovation, precision, offsets, cells, counts, tile, rows, arrived):
    pairs = (
        (counts_in, counts),
        (innovation_in, innovation),
        (precision_in, precision),
        (offsets_in, offsets),
        (cells_in, cells),
    )
    copies = [pltpu.make_async_copy(source, held, arrived.at[k]) for k, (source, held) in enumerate(pairs)]
    for copy in copies:
        copy.start()
    for copy in copies:
        copy.wait()
    slots, dests = innovation.shape
    live = lax.broadcasted_iota(jnp.int32, (slots, dests), 0) < counts[...]
    tile[0:slots, 0:dests] = jnp.where(live, innovation[...] * precision[...], 0.0)
    tile[slots : 2 * slots, 0:dests] = offsets[0]
    tile[2 * slots : 3 * slots, 0:dests] = offsets[1]
    tile[3 * slots : 4 * slots, 0:dests] = cells[...].astype(jnp.float32)
    rows[...] = tile[...].T
    for d in range(dests):
        for k in range(3):
            out[d, :, k * LANES : (k + 1) * LANES] = rows[pl.ds((d + k - 1) % dests, 1), :]


def fixed_body(std, sea, diffusivity, spread, coef, first, last, stage):
    channels, rows, cols = std.shape
    mask = sea[...].astype(jnp.float32)
    product = std[...].astype(jnp.float32) * mask[None]
    for part in range(cols // LANES):
        stage[part] = product[:, :, part * LANES : (part + 1) * LANES].reshape(channels * rows, LANES)
    coef[...] = diffusivity[...] * mask
    lane = lax.broadcasted_iota(jnp.int32, (channels, LANES), 1)
    ends = [jnp.zeros((channels, LANES), jnp.float32)] * 2
    for i in range(rows):
        here = [stage[part, pl.ds(i, channels, stride=rows), :] for part in range(cols // LANES)]
        for part, values in enumerate(here):
            spread[i, :, part * LANES : (part + 1) * LANES] = values
        inside = (lane >= RIM * i) & (lane < RIM * (i + 1))
        ends[0] = jnp.where(inside, pltpu.roll(here[0], (RIM * i) % LANES, 1), ends[0])
        ends[1] = jnp.where(inside, pltpu.roll(here[-1], (RIM * i + RIM) % LANES, 1), ends[1])
    lane_row = lax.broadcasted_iota(jnp.int32, (1, LANES), 1)
    for which, rim in enumerate((first, last)):
        edge = coef[:, 0:LANES] if which == 0 else coef[:, cols - LANES : cols]
        packed = jnp.zeros((1, LANES), jnp.float32)
        for i in range(rows):
            inside = (lane_row >= RIM * i) & (lane_row < RIM * (i + 1))
            turned = pltpu.roll(edge[i : i + 1], (RIM * i + RIM * which) % LANES, 1)
            packed = jnp.where(inside, turned, packed)
        rim[0:channels] = ends[which]
        rim[channels : channels + 8] = jnp.broadcast_to(packed, (8, LANES))


def record_fields(block, slots):
    quarter = block.shape[0] // 4
    lane = lax.broadcasted_iota(jnp.int32, (quarter, LANES), 1)
    fields = []
    for f in range(4):
        joined = None
        for b in range(4):
            part = block[b * quarter : (b + 1) * quarter]
            turn = (slots * (b - f)) % LANES
            if turn:
                part = pltpu.roll(part, turn, 1)
            joined = part if b == 0 else jnp.where(lane >= slots * b, part, joined)
        fields.append(joined)
    return fields


def build_body(arrived, spread, state, sides, whole, real, total, *held):
    rows, channels, cols = spread.shape
    slots = LANES // 4
    blocks = whole.shape[2]
    chunks = len(held) // 7
    a_high, a_low, b_high, b_low, c_both, d_high, d_low = [held[q * chunks : (q + 1) * chunks] for q in range(7)]

    for k in range(3):
        weight, east, north, cell = record_fields(arrived[:, 0, k * LANES : (k + 1) * LANES], slots)
        cell = cell.astype(jnp.int32)
        for f, values in enumerate((cell >> 12, (cell >> 8) & 15, cell & 255)):
            whole[k, f] = values
        if k == 1:
            parts = (weight * (1.0 - north), weight * north, 1.0 - east, east)
        else:
            parts = (1.0 - north, north, 1.0 - east, east, weight)
        for f, values in enumerate(parts):
            high = values.astype(jnp.bfloat16).astype(jnp.float32)
            if k == 1 or f == 4:
                real[k, 2 * f] = high
                real[k, 2 * f + 1] = values - high
            else:
                real[k, 2 * f] = values

    def pick(away, at, after):
        return jnp.where(away == 0, at, jnp.where(away == 1, after, 0.0))

    def block(n, c, here):
        row_of = lambda k, f: real[k, f, n : n + 1, :]
        index = lambda k, f, size: lax.broadcasted_iota(jnp.int32, (size, LANES), 0) - whole[k, f, n : n + 1, :]

        hot = jnp.where(index(1, 0, channels) == 0, 1.0, 0.0).astype(jnp.bfloat16)
        away = index(1, 1, rows)
        high, low = pick(away, row_of(1, 0), row_of(1, 2)), pick(away, row_of(1, 1), row_of(1, 3))
        wide = lambda x: jnp.broadcast_to(x, (channels, LANES)).astype(jnp.bfloat16)
        for row in range(rows):
            at = slice(row * channels, (row + 1) * channels)
            a_high[c][at, here] = hot * wide(high[row : row + 1])
            a_low[c][at, here] = hot * wide(low[row : row + 1])
        away = index(1, 2, cols)
        b_high[c][:, here] = pick(away, row_of(1, 4), row_of(1, 6)).astype(jnp.bfloat16)
        b_low[c][:, here] = pick(away, row_of(1, 5), row_of(1, 7)).astype(jnp.bfloat16)

        for side, (k, base) in enumerate(((0, cols - RIM), (2, 0))):
            hot = index(k, 0, channels) == 0
            for part in range(2):
                at = slice(part * channels, (part + 1) * channels)
                c_both[c][side, at, here] = jnp.where(hot, row_of(k, 8 + part), 0.0).astype(jnp.bfloat16)
            by_row = pick(index(k, 1, rows), row_of(k, 0), row_of(k, 2))
            by_col = pick(index(k, 2, RIM) + base, row_of(k, 4), row_of(k, 6))
            both = (by_row[:, None, :] * by_col[None, :, :]).reshape(rows * RIM, LANES)
            high = both.astype(jnp.bfloat16)
            d_high[c][side, :, here] = high
            d_low[c][side, :, here] = (both - high.astype(jnp.float32)).astype(jnp.bfloat16)

    dot = lambda x, y: lax.dot_general(x, y, NT, preferred_element_type=jnp.float32)
    per = blocks // chunks
    rim = [0.0, 0.0]
    for c in range(chunks):
        for n in range(per):
            block(c * per + n, c, slice(n * LANES, (n + 1) * LANES))
        first, second = b_high[c][...], b_low[c][...]
        part = dot(a_high[c][...], first) + (dot(a_high[c][...], second) + dot(a_low[c][...], first))
        total[...] = part if c == 0 else total[...] + part
        for side in range(2):
            first = dot(c_both[c][side], d_high[c][side])
            second = dot(c_both[c][side, 0:channels], d_low[c][side])
            rim[side] = rim[side] + (first[0:channels] + (first[channels:] + second))
    for side in range(2):
        sides[side] = rim[side]
    for i in range(rows):
        state[i] = total[i * channels : (i + 1) * channels, :] * spread[i]


def rim_body(state, sides, coef, rim_left, rim_right, tails, coef_out, to_up, to_down):
    rows, channels, cols = state.shape
    lane = lax.broadcasted_iota(jnp.int32, (channels, LANES), 1)
    lane_row = lax.broadcasted_iota(jnp.int32, (1, LANES), 1)

    def outer(left, right, i, lanes):
        left = pltpu.roll(left, (LANES - RIM - RIM * i) % LANES, 1)
        right = pltpu.roll(right, (LANES - RIM * i) % LANES, 1)
        return jnp.where(lanes < RIM, right, jnp.where(lanes >= LANES - RIM, left, 0.0))

    left = sides[0] * rim_left[0:channels]
    right = sides[1] * rim_right[0:channels]
    coef_out[:, 0:cols] = coef[...]
    for i in range(rows):
        tails[i] = outer(left, right, i, lane)
        coef_out[i : i + 1, cols : cols + LANES] = outer(
            rim_left[channels : channels + 1], rim_right[channels : channels + 1], i, lane_row
        )

    for out, start in ((to_down, 0), (to_up, rows - SWEEPS)):
        packed = jnp.zeros((channels, LANES), jnp.float32)
        for q in range(SWEEPS):
            i = start + q
            out[q * channels : (q + 1) * channels, :] = state[i]
            inside = (lane >= 2 * RIM * q) & (lane < 2 * RIM * (q + 1))
            packed = jnp.where(inside, pltpu.roll(tails[i], (2 * RIM * q + RIM) % LANES, 1), packed)
        base = SWEEPS * channels
        half = channels // 2
        out[base : base + half, 0:LANES] = packed[0:half]
        out[base : base + half, LANES : 2 * LANES] = packed[half:channels]
        base = base + half
        out[base : base + 8, :] = jnp.zeros((8, cols), jnp.float32)
        out[base : base + SWEEPS, :] = coef_out[start : start + SWEEPS, 0:cols]
        out[base + 8 : base + 16, :] = jnp.zeros((8, cols), jnp.float32)
        out[base + 8 : base + 8 + SWEEPS, 0:LANES] = coef_out[start : start + SWEEPS, cols : cols + LANES]


def set_faces(faces, field):
    rows, width = field.shape
    east = jnp.sqrt(field * pltpu.roll(field, width - 1, 1))
    north = jnp.sqrt(field * pltpu.roll(field, rows - 1, 0))
    west = pltpu.roll(east, 1, 1)
    south = pltpu.roll(north, 1, 0)
    faces[0, 0:rows] = 1.0 - ((east + west) + (north + south))
    for k, values in enumerate((east, west, north, south)):
        faces[1 + k, 0:rows] = values


def turns(load, count, width):
    return [[(pltpu.roll(load(r, g), width - 1, 1), pltpu.roll(load(r, g), 1, 1)) for r in range(count)] for g in range(4)]


def swept(load, turned, faces, first, store):
    width = faces.shape[2]
    for r in range(len(turned[0])):
        c, e, w, n, s = [jnp.broadcast_to(faces[k, pl.ds(first + r, 1), :], (8, width)) for k in range(5)]
        for g in range(len(turned)):
            east, west = turned[g][r]
            store(r, g, (c * load(r, g) + (e * east + w * west)) + (n * load(r + 1, g) + s * load(r - 1, g)))


def inner_body(state, tails, coef, edge_low, edge_high, middle, work, faces):
    rows, channels, cols = state.shape
    width = cols + LANES
    step = 4
    part = lambda g: slice(8 * g, 8 * (g + 1))

    set_faces(faces, coef[...])

    def fill(i, carry):
        work[0, i, :, 0:cols] = state[i]
        work[0, i, :, cols:width] = tails[i]
        return carry

    lax.fori_loop(0, rows, fill, 0)

    def sweep(t, carry):
        now, then = lax.rem(t, 2), lax.rem(t + 1, 2)
        for k in range(2):
            edge_low[t, k] = work[now, t + k]
            edge_high[t, k] = work[now, rows - 2 - t + k]

        def chunk(k, inside):
            row = t + 1 + step * k

            def store(r, g, values):
                work[then, row + r, part(g), :] = values

            load = lambda r, g: work[now, row + r, part(g), :]
            swept(load, turns(load, step, width), faces, row, store)
            return inside

        lax.fori_loop(0, lax.div(rows - 2 * (t + 1) + step - 1, step), chunk, 0)
        return carry

    lax.fori_loop(0, SWEEPS, sweep, 0)
    for k in range(rows - 2 * SWEEPS):
        middle[k] = work[SWEEPS % 2, SWEEPS + k]


def outer_body(edge_low, edge_high, middle, coef, spread, from_down, from_up, out, work_low, work_high, faces, stage):
    rows, channels, cols = spread.shape
    width = cols + LANES
    half = channels // 2
    lane = lax.broadcasted_iota(jnp.int32, (channels, LANES), 1)
    part = lambda g: slice(8 * g, 8 * (g + 1))

    stage[...] = jnp.zeros_like(stage)
    stage[SWEEPS : SWEEPS + rows, :] = coef[...]
    for block, work, start in ((from_down, work_low, 0), (from_up, work_high, SWEEPS + rows)):
        base = SWEEPS * channels
        packed = jnp.concatenate([block[base : base + half, 0:LANES], block[base : base + half, LANES : 2 * LANES]], axis=0)
        for q in range(SWEEPS):
            work[0, q, :, 0:cols] = block[q * channels : (q + 1) * channels, :]
            tail = pltpu.roll(packed, (LANES - 2 * RIM * q - RIM) % LANES, 1)
            work[0, q, :, cols:width] = jnp.where((lane < RIM) | (lane >= LANES - RIM), tail, 0.0)
        base = base + half
        stage[start : start + SWEEPS, 0:cols] = block[base : base + SWEEPS, :]
        stage[start : start + SWEEPS, cols:width] = block[base + 8 : base + 8 + SWEEPS, 0:LANES]
    set_faces(faces, stage[...])

    def sweep(t, carry):
        now, then = lax.rem(t, 2), lax.rem(t + 1, 2)

        def load_low(r, g):
            j = r + 1
            return work_low[now, j, part(g), :] if j < SWEEPS else edge_low[t, j - SWEEPS, part(g), :]

        def load_high(r, g):
            j = r + 1
            return work_high[now, j - 2, part(g), :] if j >= 2 else edge_high[t, j, part(g), :]

        def store_low(r, g, values):
            work_low[then, r, part(g), :] = values

        def store_high(r, g, values):
            work_high[then, r, part(g), :] = values

        low, high = turns(load_low, SWEEPS, width), turns(load_high, SWEEPS, width)
        swept(load_low, low, faces, t + 1, store_low)
        swept(load_high, high, faces, SWEEPS + rows - 1 - t, store_high)
        return carry

    lax.fori_loop(0, SWEEPS, sweep, 0)

    last = SWEEPS % 2
    for i in range(rows):
        if i < SWEEPS:
            done = work_low[last, i, :, 0:cols]
        elif i < rows - SWEEPS:
            done = middle[i - SWEEPS, :, 0:cols]
        else:
            done = work_high[last, i - (rows - SWEEPS), :, 0:cols]
        result = done * spread[i]
        for block in range(cols // LANES):
            first = (i // 8) * 8 * (cols // LANES) + block * 8 + i % 8
            out[pl.ds(first, channels, stride=rows * cols // LANES), :] = result[:, block * LANES : (block + 1) * LANES]


def per_device(
    obs_innovation,
    obs_precision,
    obs_offsets,
    obs_cell,
    obs_counts,
    land_sea,
    diffusivity,
    background_std,
):
    dests, slots = obs_innovation.shape[2:]
    channels, rows, cols = background_std.shape
    width = cols + LANES
    count_rows, count_cols = lax.axis_size("row"), lax.axis_size("col")
    records = dests * slots

    by_slot = lambda x: x.reshape(dests, slots).T
    offsets = obs_offsets.reshape(dests, 2, slots).transpose(1, 2, 0)
    vmem = lambda *shape: pltpu.VMEM(shape, jnp.float32)
    bf16 = lambda *shape: pltpu.VMEM(shape, jnp.bfloat16)
    packed = kernel_call(
        pack_body,
        "pack_records",
        f32(dests, 1, 3 * LANES),
        (by_slot(obs_innovation), by_slot(obs_precision), offsets, by_slot(obs_cell), obs_counts.reshape(1, dests)),
        [
            vmem(slots, dests),
            vmem(slots, dests),
            vmem(2, slots, dests),
            pltpu.VMEM((slots, dests), jnp.int32),
            pltpu.VMEM((1, dests), jnp.int32),
            vmem(LANES, LANES),
            vmem(LANES, LANES),
            pltpu.SemaphoreType.DMA((5,)),
        ],
        moved=200_000,
        place=pltpu.HBM,
        grant=ALL_VMEM_BYTES,
    )
    arrived = lax.all_to_all(packed, "col", split_axis=0, concat_axis=0, tiled=True)

    spread, coef, first, last = kernel_call(
        fixed_body,
        "fixed_fields",
        (f32(rows, channels, cols), f32(rows, cols), f32(channels + 8, LANES), f32(channels + 8, LANES)),
        (background_std, land_sea, diffusivity),
        [vmem(cols // LANES, channels * rows, LANES)],
        moved=2_000_000,
    )
    to_east = [(i, (i + 1) % count_cols) for i in range(count_cols)]
    to_west = [(j, i) for i, j in to_east]
    rim_left = lax.ppermute(last, "col", to_east)
    rim_right = lax.ppermute(first, "col", to_west)

    blocks = records // LANES
    chunks = min(CHUNKS, blocks)
    piece = records // chunks
    state, sides = kernel_call(
        build_body,
        "build_state",
        (f32(rows, channels, cols), f32(2, channels, LANES)),
        (arrived, spread),
        [pltpu.VMEM((3, 3, blocks, LANES), jnp.int32), vmem(3, 10, blocks, LANES), vmem(rows * channels, cols)]
        + [bf16(rows * channels, piece)] * (2 * chunks)
        + [bf16(cols, piece)] * (2 * chunks)
        + [bf16(2, 2 * channels, piece)] * chunks
        + [bf16(2, rows * RIM, piece)] * (2 * chunks),
        moved=10_000_000,
    )
    slab = SWEEPS * channels + channels // 2 + 16
    tails, coef_wide, to_up, to_down = kernel_call(
        rim_body,
        "build_rims",
        (f32(rows, channels, LANES), f32(rows, width), f32(slab, cols), f32(slab, cols)),
        (state, sides, coef, rim_left, rim_right),
        moved=2_000_000,
    )
    up = [(i, i + 1) for i in range(count_rows - 1)]
    down = [(j, i) for i, j in up]
    from_down = lax.ppermute(to_up, "row", up)
    from_up = lax.ppermute(to_down, "row", down)

    edge_low, edge_high, middle = kernel_call(
        inner_body,
        "inner_sweeps",
        (
            f32(SWEEPS, 2, channels, width),
            f32(SWEEPS, 2, channels, width),
            f32(rows - 2 * SWEEPS, channels, width),
        ),
        (state, tails, coef_wide),
        [vmem(2, rows + 4, channels, width), vmem(5, rows + 4, width)],
        moved=6_000_000,
    )
    depth = (rows + 2 * SWEEPS + 7) // 8 * 8
    out = kernel_call(
        outer_body,
        "outer_sweeps",
        f32(channels * rows * cols // LANES, LANES),
        (edge_low, edge_high, middle, coef_wide, spread, from_down, from_up),
        [vmem(2, SWEEPS, channels, width)] * 2 + [vmem(5, depth, width), vmem(depth, width)],
        moved=10_000_000,
    )
    out = out.reshape(channels, rows // 8, cols // LANES, 8, LANES)
    return out.transpose(0, 1, 3, 2, 4).reshape(channels, rows, cols)


def solution(mesh):
    placed = (
        P("row", "col", None, None),
        P("row", "col", None, None),
        P("row", "col", None, None, None),
        P("row", "col", None, None),
        P("row", "col", None),
        P("row", "col"),
        P("row", "col"),
        P(None, "row", "col"),
    )
    return jax.shard_map(
        per_device, mesh=mesh, in_specs=placed, out_specs=P(None, "row", "col"), check_vma=False
    )
```

```python
import functools

import jax
import jax.numpy as jnp
from jax import lax
from jax.experimental import pallas as pl
from jax.experimental.pallas import tpu as pltpu
from jax.sharding import PartitionSpec as P

SWEEPS = 6
LANES = 128
CHUNKS = 4
RIM = 8
VMEM_BYTES = 24 * 1024 * 1024
ALL_VMEM_BYTES = 58 * 1024 * 1024

NT = (((1,), (1,)), ((), ()))


def kernel_call(body, name, outs, inputs, scratch=(), moved=0, place=pltpu.VMEM, grant=VMEM_BYTES, held=(), out_place=pltpu.VMEM):
    specs = [pl.BlockSpec(memory_space=out_place if k in held else place) for k in range(len(inputs))]
    return pl.pallas_call(
        body,
        name=name,
        out_shape=outs,
        in_specs=specs,
        out_specs=jax.tree.map(lambda _: pl.BlockSpec(memory_space=out_place), outs),
        scratch_shapes=list(scratch),
        input_output_aliases={k: 0 for k in held},
        compiler_params=pltpu.CompilerParams(vmem_limit_bytes=grant),
        cost_estimate=pl.CostEstimate(flops=0, bytes_accessed=moved, transcendentals=0),
    )(*inputs)


def f32(*shape):
    return jax.ShapeDtypeStruct(shape, jnp.float32)


def pack_body(innovation_in, precision_in, offsets_in, cells_in, counts_in, out, innovation, precision, offsets, cells, counts, tile, rows, arrived):
    pairs = (
        (counts_in, counts),
        (innovation_in, innovation),
        (precision_in, precision),
        (offsets_in, offsets),
        (cells_in, cells),
    )
    copies = [pltpu.make_async_copy(source, held, arrived.at[k]) for k, (source, held) in enumerate(pairs)]
    for copy in copies:
        copy.start()
    for copy in copies:
        copy.wait()
    slots, dests = innovation.shape
    live = lax.broadcasted_iota(jnp.int32, (slots, dests), 0) < counts[...]
    tile[0:slots, 0:dests] = jnp.where(live, innovation[...] * precision[...], 0.0)
    tile[slots : 2 * slots, 0:dests] = offsets[0]
    tile[2 * slots : 3 * slots, 0:dests] = offsets[1]
    tile[3 * slots : 4 * slots, 0:dests] = cells[...].astype(jnp.float32)
    rows[...] = tile[...].T
    for d in range(dests):
        for k in range(3):
            out[d, :, k * LANES : (k + 1) * LANES] = rows[pl.ds((d + k - 1) % dests, 1), :]


def fixed_body(std, sea, diffusivity, spread, coef, first, last, stage):
    channels, rows, cols = std.shape
    mask = sea[...].astype(jnp.float32)
    product = std[...].astype(jnp.float32) * mask[None]
    for part in range(cols // LANES):
        stage[part] = product[:, :, part * LANES : (part + 1) * LANES].reshape(channels * rows, LANES)
    coef[...] = diffusivity[...] * mask
    lane = lax.broadcasted_iota(jnp.int32, (channels, LANES), 1)
    ends = [jnp.zeros((channels, LANES), jnp.float32)] * 2
    for i in range(rows):
        here = [stage[part, pl.ds(i, channels, stride=rows), :] for part in range(cols // LANES)]
        for part, values in enumerate(here):
            spread[i, :, part * LANES : (part + 1) * LANES] = values
        inside = (lane >= RIM * i) & (lane < RIM * (i + 1))
        ends[0] = jnp.where(inside, pltpu.roll(here[0], (RIM * i) % LANES, 1), ends[0])
        ends[1] = jnp.where(inside, pltpu.roll(here[-1], (RIM * i + RIM) % LANES, 1), ends[1])
    lane_row = lax.broadcasted_iota(jnp.int32, (1, LANES), 1)
    for which, rim in enumerate((first, last)):
        edge = coef[:, 0:LANES] if which == 0 else coef[:, cols - LANES : cols]
        packed = jnp.zeros((1, LANES), jnp.float32)
        for i in range(rows):
            inside = (lane_row >= RIM * i) & (lane_row < RIM * (i + 1))
            turned = pltpu.roll(edge[i : i + 1], (RIM * i + RIM * which) % LANES, 1)
            packed = jnp.where(inside, turned, packed)
        rim[0:channels] = ends[which]
        rim[channels : channels + 8] = jnp.broadcast_to(packed, (8, LANES))


def record_fields(block, slots):
    quarter = block.shape[0] // 4
    lane = lax.broadcasted_iota(jnp.int32, (quarter, LANES), 1)
    fields = []
    for f in range(4):
        joined = None
        for b in range(4):
            part = block[b * quarter : (b + 1) * quarter]
            turn = (slots * (b - f)) % LANES
            if turn:
                part = pltpu.roll(part, turn, 1)
            joined = part if b == 0 else jnp.where(lane >= slots * b, part, joined)
        fields.append(joined)
    return fields


def build_body(arrived, spread, state, sides, whole, real, total, *held):
    rows, channels, cols = spread.shape
    slots = LANES // 4
    blocks = whole.shape[2]
    chunks = len(held) // 7
    a_high, a_low, b_high, b_low, c_both, d_high, d_low = [held[q * chunks : (q + 1) * chunks] for q in range(7)]

    for k in range(3):
        weight, east, north, cell = record_fields(arrived[:, 0, k * LANES : (k + 1) * LANES], slots)
        cell = cell.astype(jnp.int32)
        for f, values in enumerate((cell >> 12, (cell >> 8) & 15, cell & 255)):
            whole[k, f] = values
        if k == 1:
            parts = (weight * (1.0 - north), weight * north, 1.0 - east, east)
        else:
            parts = (1.0 - north, north, 1.0 - east, east, weight)
        for f, values in enumerate(parts):
            high = values.astype(jnp.bfloat16).astype(jnp.float32)
            if k == 1 or f == 4:
                real[k, 2 * f] = high
                real[k, 2 * f + 1] = values - high
            else:
                real[k, 2 * f] = values

    def pick(away, at, after):
        return jnp.where(away == 0, at, jnp.where(away == 1, after, 0.0))

    def block(n, c, here):
        row_of = lambda k, f: real[k, f, n : n + 1, :]
        index = lambda k, f, size: lax.broadcasted_iota(jnp.int32, (size, LANES), 0) - whole[k, f, n : n + 1, :]

        hot = jnp.where(index(1, 0, channels) == 0, 1.0, 0.0).astype(jnp.bfloat16)
        away = index(1, 1, rows)
        high, low = pick(away, row_of(1, 0), row_of(1, 2)), pick(away, row_of(1, 1), row_of(1, 3))
        wide = lambda x: jnp.broadcast_to(x, (channels, LANES)).astype(jnp.bfloat16)
        for row in range(rows):
            at = slice(row * channels, (row + 1) * channels)
            a_high[c][at, here] = hot * wide(high[row : row + 1])
            a_low[c][at, here] = hot * wide(low[row : row + 1])
        away = index(1, 2, cols)
        b_high[c][:, here] = pick(away, row_of(1, 4), row_of(1, 6)).astype(jnp.bfloat16)
        b_low[c][:, here] = pick(away, row_of(1, 5), row_of(1, 7)).astype(jnp.bfloat16)

        for side, (k, base) in enumerate(((0, cols - RIM), (2, 0))):
            hot = index(k, 0, channels) == 0
            for part in range(2):
                at = slice(part * channels, (part + 1) * channels)
                c_both[c][side, at, here] = jnp.where(hot, row_of(k, 8 + part), 0.0).astype(jnp.bfloat16)
            by_row = pick(index(k, 1, rows), row_of(k, 0), row_of(k, 2))
            by_col = pick(index(k, 2, RIM) + base, row_of(k, 4), row_of(k, 6))
            both = (by_row[:, None, :] * by_col[None, :, :]).reshape(rows * RIM, LANES)
            high = both.astype(jnp.bfloat16)
            d_high[c][side, :, here] = high
            d_low[c][side, :, here] = (both - high.astype(jnp.float32)).astype(jnp.bfloat16)

    dot = lambda x, y: lax.dot_general(x, y, NT, preferred_element_type=jnp.float32)
    per = blocks // chunks
    rim = [0.0, 0.0]
    for c in range(chunks):
        for n in range(per):
            block(c * per + n, c, slice(n * LANES, (n + 1) * LANES))
        first, second = b_high[c][...], b_low[c][...]
        part = dot(a_high[c][...], first) + (dot(a_high[c][...], second) + dot(a_low[c][...], first))
        total[...] = part if c == 0 else total[...] + part
        for side in range(2):
            first = dot(c_both[c][side], d_high[c][side])
            second = dot(c_both[c][side, 0:channels], d_low[c][side])
            rim[side] = rim[side] + (first[0:channels] + (first[channels:] + second))
    for side in range(2):
        sides[side] = rim[side]
    for i in range(rows):
        state[i] = total[i * channels : (i + 1) * channels, :] * spread[i]


def rim_body(state, sides, coef, rim_left, rim_right, tails, coef_out, to_up, to_down):
    rows, channels, cols = state.shape
    lane = lax.broadcasted_iota(jnp.int32, (channels, LANES), 1)
    lane_row = lax.broadcasted_iota(jnp.int32, (1, LANES), 1)

    def outer(left, right, i, lanes):
        left = pltpu.roll(left, (LANES - RIM - RIM * i) % LANES, 1)
        right = pltpu.roll(right, (LANES - RIM * i) % LANES, 1)
        return jnp.where(lanes < RIM, right, jnp.where(lanes >= LANES - RIM, left, 0.0))

    left = sides[0] * rim_left[0:channels]
    right = sides[1] * rim_right[0:channels]
    coef_out[:, 0:cols] = coef[...]
    for i in range(rows):
        tails[i] = outer(left, right, i, lane)
        coef_out[i : i + 1, cols : cols + LANES] = outer(
            rim_left[channels : channels + 1], rim_right[channels : channels + 1], i, lane_row
        )

    for out, start in ((to_down, 0), (to_up, rows - SWEEPS)):
        packed = jnp.zeros((channels, LANES), jnp.float32)
        for q in range(SWEEPS):
            i = start + q
            out[q * channels : (q + 1) * channels, :] = state[i]
            inside = (lane >= 2 * RIM * q) & (lane < 2 * RIM * (q + 1))
            packed = jnp.where(inside, pltpu.roll(tails[i], (2 * RIM * q + RIM) % LANES, 1), packed)
        base = SWEEPS * channels
        half = channels // 2
        out[base : base + half, 0:LANES] = packed[0:half]
        out[base : base + half, LANES : 2 * LANES] = packed[half:channels]
        base = base + half
        out[base : base + 8, :] = jnp.zeros((8, cols), jnp.float32)
        out[base : base + SWEEPS, :] = coef_out[start : start + SWEEPS, 0:cols]
        out[base + 8 : base + 16, :] = jnp.zeros((8, cols), jnp.float32)
        out[base + 8 : base + 8 + SWEEPS, 0:LANES] = coef_out[start : start + SWEEPS, cols : cols + LANES]


def set_faces(faces, field):
    rows, width = field.shape
    east = jnp.sqrt(field * pltpu.roll(field, width - 1, 1))
    north = jnp.sqrt(field * pltpu.roll(field, rows - 1, 0))
    west = pltpu.roll(east, 1, 1)
    south = pltpu.roll(north, 1, 0)
    faces[0, 0:rows] = 1.0 - ((east + west) + (north + south))
    for k, values in enumerate((east, west, north, south)):
        faces[1 + k, 0:rows] = values


def turns(load, count, width):
    return [[(pltpu.roll(load(r, g), width - 1, 1), pltpu.roll(load(r, g), 1, 1)) for r in range(count)] for g in range(4)]


def swept(load, turned, faces, first, store):
    width = faces.shape[2]
    for r in range(len(turned[0])):
        c, e, w, n, s = [jnp.broadcast_to(faces[k, pl.ds(first + r, 1), :], (8, width)) for k in range(5)]
        for g in range(len(turned)):
            east, west = turned[g][r]
            store(r, g, (c * load(r, g) + (e * east + w * west)) + (n * load(r + 1, g) + s * load(r - 1, g)))


def side_by_side(state, tails, i, g):
    here = slice(8 * g, 8 * (g + 1))
    return jnp.concatenate([state[i, here, :], tails[i, here, :]], axis=1)


def inner_body(state, tails, coef, edge_low, edge_high, middle, work, faces):
    rows, channels, cols = state.shape
    width = cols + LANES
    part = lambda g: slice(8 * g, 8 * (g + 1))

    set_faces(faces, coef[...])
    for g in range(channels // 8):
        for k in range(2):
            edge_low[0, k, part(g), :] = side_by_side(state, tails, k, g)
            edge_high[0, k, part(g), :] = side_by_side(state, tails, rows - 2 + k, g)

    def loader(t):
        if t == 0:
            return lambda r, g: side_by_side(state, tails, 1 + r, g)
        return lambda r, g: work[t % 2, t + 1 + r, part(g), :]

    def storer(t):
        def store(r, g, values):
            done, row = t + 1, t + 1 + r
            if done == SWEEPS:
                middle[r, part(g), :] = values
                return
            work[done % 2, row, part(g), :] = values
            if row < done + 2:
                edge_low[done, row - done, part(g), :] = values
            if row >= rows - 2 - done:
                edge_high[done, row - (rows - 2 - done), part(g), :] = values

        return store

    for t in range(SWEEPS):
        load, count = loader(t), rows - 2 * (t + 1)
        swept(load, turns(load, count, width), faces, t + 1, storer(t))


def side_body(low, edge, middle, coef, spread, block, *rest):
    out, work, faces, stage, result, sent = rest[-6:]
    rows, channels, cols = spread.shape
    width = cols + LANES
    half = channels // 2
    keep = rows - SWEEPS
    lane = lax.broadcasted_iota(jnp.int32, (channels, LANES), 1)
    part = lambda g: slice(8 * g, 8 * (g + 1))

    base = SWEEPS * channels
    packed = jnp.concatenate([block[base : base + half, 0:LANES], block[base : base + half, LANES : 2 * LANES]], axis=0)
    for q in range(SWEEPS):
        work[0, q, :, 0:cols] = block[q * channels : (q + 1) * channels, :]
        tail = pltpu.roll(packed, (LANES - 2 * RIM * q - RIM) % LANES, 1)
        work[0, q, :, cols:width] = jnp.where((lane < RIM) | (lane >= LANES - RIM), tail, 0.0)
    base = base + half
    start = 0 if low else keep
    stage[start : start + SWEEPS, 0:cols] = block[base : base + SWEEPS, :]
    stage[start : start + SWEEPS, cols:width] = block[base + 8 : base + 8 + SWEEPS, 0:LANES]
    if low:
        stage[SWEEPS:rows, :] = coef[0:keep, :]
    else:
        stage[0:keep, :] = coef[SWEEPS:rows, :]
    set_faces(faces, stage[...])

    def loader(t):
        def load(r, g):
            j = r + 1 if low else r - 1
            if 0 <= j < SWEEPS:
                return work[t % 2, j, part(g), :]
            return edge[t, j - SWEEPS if low else r + 1, part(g), :]

        return load

    def storer(t):
        def store(r, g, values):
            work[(t + 1) % 2, r, part(g), :] = values

        return store

    for t in range(SWEEPS):
        load = loader(t)
        swept(load, turns(load, SWEEPS, width), faces, t + 1 if low else keep - 1 - t, storer(t))

    for i in range(0 if low else rows // 2, rows // 2 if low else rows):
        if SWEEPS <= i < keep:
            done = middle[i - SWEEPS, :, 0:cols]
        else:
            done = work[SWEEPS % 2, i if low else i - keep, :, 0:cols]
        done = done * spread[i]
        for k in range(cols // LANES):
            first = k * 8 + i % 8
            result[pl.ds(first, channels, stride=rows // 2 * cols // LANES), :] = done[:, k * LANES : (k + 1) * LANES]
    size = rows // 2 * cols // LANES
    target = out.at[:, 0:size, :] if low else out.at[:, size : 2 * size, :]
    copy = pltpu.make_async_copy(result.reshape(channels, size, LANES), target, sent)
    copy.start()
    copy.wait()


def per_device(
    obs_innovation,
    obs_precision,
    obs_offsets,
    obs_cell,
    obs_counts,
    land_sea,
    diffusivity,
    background_std,
):
    dests, slots = obs_innovation.shape[2:]
    channels, rows, cols = background_std.shape
    width = cols + LANES
    count_rows, count_cols = lax.axis_size("row"), lax.axis_size("col")
    records = dests * slots

    by_slot = lambda x: x.reshape(dests, slots).T
    offsets = obs_offsets.reshape(dests, 2, slots).transpose(1, 2, 0)
    vmem = lambda *shape: pltpu.VMEM(shape, jnp.float32)
    bf16 = lambda *shape: pltpu.VMEM(shape, jnp.bfloat16)
    packed = kernel_call(
        pack_body,
        "pack_records",
        f32(dests, 1, 3 * LANES),
        (by_slot(obs_innovation), by_slot(obs_precision), offsets, by_slot(obs_cell), obs_counts.reshape(1, dests)),
        [
            vmem(slots, dests),
            vmem(slots, dests),
            vmem(2, slots, dests),
            pltpu.VMEM((slots, dests), jnp.int32),
            pltpu.VMEM((1, dests), jnp.int32),
            vmem(LANES, LANES),
            vmem(LANES, LANES),
            pltpu.SemaphoreType.DMA((5,)),
        ],
        moved=200_000,
        place=pltpu.HBM,
        grant=ALL_VMEM_BYTES,
    )
    arrived = lax.all_to_all(packed, "col", split_axis=0, concat_axis=0, tiled=True)

    spread, coef, first, last = kernel_call(
        fixed_body,
        "fixed_fields",
        (f32(rows, channels, cols), f32(rows, cols), f32(channels + 8, LANES), f32(channels + 8, LANES)),
        (background_std, land_sea, diffusivity),
        [vmem(cols // LANES, channels * rows, LANES)],
        moved=2_000_000,
    )
    to_east = [(i, (i + 1) % count_cols) for i in range(count_cols)]
    to_west = [(j, i) for i, j in to_east]
    rim_left = lax.ppermute(last, "col", to_east)
    rim_right = lax.ppermute(first, "col", to_west)

    blocks = records // LANES
    chunks = min(CHUNKS, blocks)
    piece = records // chunks
    state, sides = kernel_call(
        build_body,
        "build_state",
        (f32(rows, channels, cols), f32(2, channels, LANES)),
        (arrived, spread),
        [pltpu.VMEM((3, 3, blocks, LANES), jnp.int32), vmem(3, 10, blocks, LANES), vmem(rows * channels, cols)]
        + [bf16(rows * channels, piece)] * (2 * chunks)
        + [bf16(cols, piece)] * (2 * chunks)
        + [bf16(2, 2 * channels, piece)] * chunks
        + [bf16(2, rows * RIM, piece)] * (2 * chunks),
        moved=10_000_000,
    )
    slab = SWEEPS * channels + channels // 2 + 16
    tails, coef_wide, to_up, to_down = kernel_call(
        rim_body,
        "build_rims",
        (f32(rows, channels, LANES), f32(rows, width), f32(slab, cols), f32(slab, cols)),
        (state, sides, coef, rim_left, rim_right),
        moved=2_000_000,
    )
    up = [(i, i + 1) for i in range(count_rows - 1)]
    down = [(j, i) for i, j in up]
    from_down = lax.ppermute(to_up, "row", up)
    from_up = lax.ppermute(to_down, "row", down)

    edge_low, edge_high, middle = kernel_call(
        inner_body,
        "inner_sweeps",
        (
            f32(SWEEPS, 2, channels, width),
            f32(SWEEPS, 2, channels, width),
            f32(rows - 2 * SWEEPS, channels, width),
        ),
        (state, tails, coef_wide),
        [vmem(2, rows, channels, width), vmem(5, rows, width)],
        moved=6_000_000,
    )
    size = rows * cols // LANES
    out = None
    for low, edge, block in ((True, edge_low, from_down), (False, edge_high, from_up)):
        out = kernel_call(
            functools.partial(side_body, low),
            "low_sweeps" if low else "high_sweeps",
            f32(channels, size, LANES),
            (edge, middle, coef_wide, spread, block) + (() if low else (out,)),
            [
                vmem(2, SWEEPS, channels, width),
                vmem(5, rows, width),
                vmem(rows, width),
                vmem(channels * size // 2, LANES),
                pltpu.SemaphoreType.DMA,
            ],
            moved=5_000_000,
            held=() if low else (5,),
            out_place=pltpu.HBM,
        )
    out = out.reshape(channels, rows // 8, cols // LANES, 8, LANES)
    return out.transpose(0, 1, 3, 2, 4).reshape(channels, rows, cols)


def solution(mesh):
    placed = (
        P("row", "col", None, None),
        P("row", "col", None, None),
        P("row", "col", None, None, None),
        P("row", "col", None, None),
        P("row", "col", None),
        P("row", "col"),
        P("row", "col"),
        P(None, "row", "col"),
    )
    return jax.shard_map(
        per_device, mesh=mesh, in_specs=placed, out_specs=P(None, "row", "col"), check_vma=False
    )
```

```python
import functools

import jax
import jax.numpy as jnp
from jax import lax
from jax.experimental import pallas as pl
from jax.experimental.pallas import tpu as pltpu
from jax.sharding import PartitionSpec as P

SWEEPS = 6
LANES = 128
CHUNKS = 4
RIM = 8
VMEM_BYTES = 24 * 1024 * 1024
ALL_VMEM_BYTES = 58 * 1024 * 1024

NT = (((1,), (1,)), ((), ()))


def kernel_call(body, name, outs, inputs, scratch=(), moved=0, place=pltpu.VMEM, grant=VMEM_BYTES, held=(), out_place=pltpu.VMEM):
    specs = [pl.BlockSpec(memory_space=out_place if k in held else place) for k in range(len(inputs))]
    return pl.pallas_call(
        body,
        name=name,
        out_shape=outs,
        in_specs=specs,
        out_specs=jax.tree.map(lambda _: pl.BlockSpec(memory_space=out_place), outs),
        scratch_shapes=list(scratch),
        input_output_aliases={k: 0 for k in held},
        compiler_params=pltpu.CompilerParams(vmem_limit_bytes=grant),
        cost_estimate=pl.CostEstimate(flops=0, bytes_accessed=moved, transcendentals=0),
    )(*inputs)


def f32(*shape):
    return jax.ShapeDtypeStruct(shape, jnp.float32)


def pack_body(innovation_in, precision_in, offsets_in, cells_in, counts_in, out, innovation, precision, offsets, cells, counts, tile, rows, arrived):
    pairs = (
        (counts_in, counts),
        (innovation_in, innovation),
        (precision_in, precision),
        (offsets_in, offsets),
        (cells_in, cells),
    )
    copies = [pltpu.make_async_copy(source, held, arrived.at[k]) for k, (source, held) in enumerate(pairs)]
    for copy in copies:
        copy.start()
    for copy in copies:
        copy.wait()
    slots, dests = innovation.shape
    live = lax.broadcasted_iota(jnp.int32, (slots, dests), 0) < counts[...]
    tile[0:slots, 0:dests] = jnp.where(live, innovation[...] * precision[...], 0.0)
    tile[slots : 2 * slots, 0:dests] = offsets[0]
    tile[2 * slots : 3 * slots, 0:dests] = offsets[1]
    tile[3 * slots : 4 * slots, 0:dests] = cells[...].astype(jnp.float32)
    rows[...] = tile[...].T
    for d in range(dests):
        for k in range(3):
            out[dests - 1 - d, :, k * LANES : (k + 1) * LANES] = rows[pl.ds((d + k - 1) % dests, 1), :]


def odd_column():
    return lax.rem(lax.axis_index("col"), 2) == 1


def fixed_body(std, sea, diffusivity, spread, coef, near, far, stage):
    channels, rows, cols = std.shape
    mask = sea[...].astype(jnp.float32)
    product = std[...].astype(jnp.float32) * mask[None]
    for part in range(cols // LANES):
        stage[part] = product[:, :, part * LANES : (part + 1) * LANES].reshape(channels * rows, LANES)
    coef[...] = diffusivity[...] * mask
    lane = lax.broadcasted_iota(jnp.int32, (channels, LANES), 1)
    ends = [jnp.zeros((channels, LANES), jnp.float32)] * 2
    for i in range(rows):
        here = [stage[part, pl.ds(i, channels, stride=rows), :] for part in range(cols // LANES)]
        for part, values in enumerate(here):
            spread[i, :, part * LANES : (part + 1) * LANES] = values
        inside = (lane >= RIM * i) & (lane < RIM * (i + 1))
        ends[0] = jnp.where(inside, pltpu.roll(here[0], (RIM * i) % LANES, 1), ends[0])
        ends[1] = jnp.where(inside, pltpu.roll(here[-1], (RIM * i + RIM) % LANES, 1), ends[1])
    lane_row = lax.broadcasted_iota(jnp.int32, (1, LANES), 1)
    for which in range(2):
        edge = coef[:, 0:LANES] if which == 0 else coef[:, cols - LANES : cols]
        packed = jnp.zeros((1, LANES), jnp.float32)
        for i in range(rows):
            inside = (lane_row >= RIM * i) & (lane_row < RIM * (i + 1))
            turned = pltpu.roll(edge[i : i + 1], (RIM * i + RIM * which) % LANES, 1)
            packed = jnp.where(inside, turned, packed)
        ends[which] = jnp.concatenate([ends[which], jnp.broadcast_to(packed, (8, LANES))], axis=0)
    odd = odd_column()
    near[...] = jnp.where(odd, ends[0], ends[1])
    far[...] = jnp.where(odd, ends[1], ends[0])


def record_fields(block, slots):
    quarter = block.shape[0] // 4
    lane = lax.broadcasted_iota(jnp.int32, (quarter, LANES), 1)
    fields = []
    for f in range(4):
        joined = None
        for b in range(4):
            part = block[b * quarter : (b + 1) * quarter]
            turn = (slots * (b - f)) % LANES
            if turn:
                part = pltpu.roll(part, turn, 1)
            joined = part if b == 0 else jnp.where(lane >= slots * b, part, joined)
        fields.append(joined)
    return fields


def build_body(arrived, spread, state, sides, whole, real, total, *held):
    rows, channels, cols = spread.shape
    slots = LANES // 4
    blocks = whole.shape[2]
    chunks = len(held) // 7
    a_high, a_low, b_high, b_low, c_both, d_high, d_low = [held[q * chunks : (q + 1) * chunks] for q in range(7)]

    for k in range(3):
        weight, east, north, cell = record_fields(arrived[:, 0, k * LANES : (k + 1) * LANES], slots)
        cell = cell.astype(jnp.int32)
        for f, values in enumerate((cell >> 12, (cell >> 8) & 15, cell & 255)):
            whole[k, f] = values
        if k == 1:
            parts = (weight * (1.0 - north), weight * north, 1.0 - east, east)
        else:
            parts = (1.0 - north, north, 1.0 - east, east, weight)
        for f, values in enumerate(parts):
            high = values.astype(jnp.bfloat16).astype(jnp.float32)
            if k == 1 or f == 4:
                real[k, 2 * f] = high
                real[k, 2 * f + 1] = values - high
            else:
                real[k, 2 * f] = values

    def pick(away, at, after):
        return jnp.where(away == 0, at, jnp.where(away == 1, after, 0.0))

    def block(n, c, here):
        row_of = lambda k, f: real[k, f, n : n + 1, :]
        index = lambda k, f, size: lax.broadcasted_iota(jnp.int32, (size, LANES), 0) - whole[k, f, n : n + 1, :]

        hot = jnp.where(index(1, 0, channels) == 0, 1.0, 0.0).astype(jnp.bfloat16)
        away = index(1, 1, rows)
        high, low = pick(away, row_of(1, 0), row_of(1, 2)), pick(away, row_of(1, 1), row_of(1, 3))
        wide = lambda x: jnp.broadcast_to(x, (channels, LANES)).astype(jnp.bfloat16)
        for row in range(rows):
            at = slice(row * channels, (row + 1) * channels)
            a_high[c][at, here] = hot * wide(high[row : row + 1])
            a_low[c][at, here] = hot * wide(low[row : row + 1])
        away = index(1, 2, cols)
        b_high[c][:, here] = pick(away, row_of(1, 4), row_of(1, 6)).astype(jnp.bfloat16)
        b_low[c][:, here] = pick(away, row_of(1, 5), row_of(1, 7)).astype(jnp.bfloat16)

        for side, (k, base) in enumerate(((0, cols - RIM), (2, 0))):
            hot = index(k, 0, channels) == 0
            for part in range(2):
                at = slice(part * channels, (part + 1) * channels)
                c_both[c][side, at, here] = jnp.where(hot, row_of(k, 8 + part), 0.0).astype(jnp.bfloat16)
            by_row = pick(index(k, 1, rows), row_of(k, 0), row_of(k, 2))
            by_col = pick(index(k, 2, RIM) + base, row_of(k, 4), row_of(k, 6))
            both = (by_row[:, None, :] * by_col[None, :, :]).reshape(rows * RIM, LANES)
            high = both.astype(jnp.bfloat16)
            d_high[c][side, :, here] = high
            d_low[c][side, :, here] = (both - high.astype(jnp.float32)).astype(jnp.bfloat16)

    dot = lambda x, y: lax.dot_general(x, y, NT, preferred_element_type=jnp.float32)
    per = blocks // chunks
    rim = [0.0, 0.0]
    for c in range(chunks):
        for n in range(per):
            block(c * per + n, c, slice(n * LANES, (n + 1) * LANES))
        first, second = b_high[c][...], b_low[c][...]
        part = dot(a_high[c][...], first) + (dot(a_high[c][...], second) + dot(a_low[c][...], first))
        total[...] = part if c == 0 else total[...] + part
        for side in range(2):
            first = dot(c_both[c][side], d_high[c][side])
            second = dot(c_both[c][side, 0:channels], d_low[c][side])
            rim[side] = rim[side] + (first[0:channels] + (first[channels:] + second))
    for side in range(2):
        sides[side] = rim[side]
    for i in range(rows):
        state[i] = total[i * channels : (i + 1) * channels, :] * spread[i]


def rim_body(state, sides, coef, near, far, tails, coef_out, to_up, to_down):
    rows, channels, cols = state.shape
    lane = lax.broadcasted_iota(jnp.int32, (channels, LANES), 1)
    lane_row = lax.broadcasted_iota(jnp.int32, (1, LANES), 1)

    def outer(left, right, i, lanes):
        left = pltpu.roll(left, (LANES - RIM - RIM * i) % LANES, 1)
        right = pltpu.roll(right, (LANES - RIM * i) % LANES, 1)
        return jnp.where(lanes < RIM, right, jnp.where(lanes >= LANES - RIM, left, 0.0))

    odd = odd_column()
    rim_left = jnp.where(odd, near[...], far[...])
    rim_right = jnp.where(odd, far[...], near[...])
    left = sides[0] * rim_left[0:channels]
    right = sides[1] * rim_right[0:channels]
    coef_out[:, 0:cols] = coef[...]
    for i in range(rows):
        tails[i] = outer(left, right, i, lane)
        coef_out[i : i + 1, cols : cols + LANES] = outer(
            rim_left[channels : channels + 1], rim_right[channels : channels + 1], i, lane_row
        )

    for out, start in ((to_down, 0), (to_up, rows - SWEEPS)):
        packed = jnp.zeros((channels, LANES), jnp.float32)
        for q in range(SWEEPS):
            i = start + q
            out[q * channels : (q + 1) * channels, :] = state[i]
            inside = (lane >= 2 * RIM * q) & (lane < 2 * RIM * (q + 1))
            packed = jnp.where(inside, pltpu.roll(tails[i], (2 * RIM * q + RIM) % LANES, 1), packed)
        base = SWEEPS * channels
        half = channels // 2
        out[base : base + half, 0:LANES] = packed[0:half]
        out[base : base + half, LANES : 2 * LANES] = packed[half:channels]
        base = base + half
        out[base : base + 8, :] = jnp.zeros((8, cols), jnp.float32)
        out[base : base + SWEEPS, :] = coef_out[start : start + SWEEPS, 0:cols]
        out[base + 8 : base + 16, :] = jnp.zeros((8, cols), jnp.float32)
        out[base + 8 : base + 8 + SWEEPS, 0:LANES] = coef_out[start : start + SWEEPS, cols : cols + LANES]


def set_faces(faces, field):
    rows, width = field.shape
    east = jnp.sqrt(field * pltpu.roll(field, width - 1, 1))
    north = jnp.sqrt(field * pltpu.roll(field, rows - 1, 0))
    west = pltpu.roll(east, 1, 1)
    south = pltpu.roll(north, 1, 0)
    faces[0, 0:rows] = 1.0 - ((east + west) + (north + south))
    for k, values in enumerate((east, west, north, south)):
        faces[1 + k, 0:rows] = values


def turns(load, count, width):
    return [[(pltpu.roll(load(r, g), width - 1, 1), pltpu.roll(load(r, g), 1, 1)) for r in range(count)] for g in range(4)]


def swept(load, turned, faces, first, store):
    width = faces.shape[2]
    for r in range(len(turned[0])):
        c, e, w, n, s = [jnp.broadcast_to(faces[k, pl.ds(first + r, 1), :], (8, width)) for k in range(5)]
        for g in range(len(turned)):
            east, west = turned[g][r]
            store(r, g, (c * load(r, g) + (e * east + w * west)) + (n * load(r + 1, g) + s * load(r - 1, g)))


def side_by_side(state, tails, i, g):
    here = slice(8 * g, 8 * (g + 1))
    return jnp.concatenate([state[i, here, :], tails[i, here, :]], axis=1)


def inner_body(state, tails, coef, edge_low, edge_high, middle, work, faces):
    rows, channels, cols = state.shape
    width = cols + LANES
    part = lambda g: slice(8 * g, 8 * (g + 1))

    set_faces(faces, coef[...])
    for g in range(channels // 8):
        for k in range(2):
            edge_low[0, k, part(g), :] = side_by_side(state, tails, k, g)
            edge_high[0, k, part(g), :] = side_by_side(state, tails, rows - 2 + k, g)

    def loader(t):
        if t == 0:
            return lambda r, g: side_by_side(state, tails, 1 + r, g)
        return lambda r, g: work[t % 2, t + 1 + r, part(g), :]

    def storer(t):
        def store(r, g, values):
            done, row = t + 1, t + 1 + r
            if done == SWEEPS:
                middle[r, part(g), :] = values
                return
            work[done % 2, row, part(g), :] = values
            if row < done + 2:
                edge_low[done, row - done, part(g), :] = values
            if row >= rows - 2 - done:
                edge_high[done, row - (rows - 2 - done), part(g), :] = values

        return store

    for t in range(SWEEPS):
        load, count = loader(t), rows - 2 * (t + 1)
        swept(load, turns(load, count, width), faces, t + 1, storer(t))


def side_body(low, edge, middle, coef, spread, block, *rest):
    out, work, faces, stage, result, sent = rest[-6:]
    rows, channels, cols = spread.shape
    width = cols + LANES
    half = channels // 2
    keep = rows - SWEEPS
    lane = lax.broadcasted_iota(jnp.int32, (channels, LANES), 1)
    part = lambda g: slice(8 * g, 8 * (g + 1))

    base = SWEEPS * channels
    packed = jnp.concatenate([block[base : base + half, 0:LANES], block[base : base + half, LANES : 2 * LANES]], axis=0)
    for q in range(SWEEPS):
        work[0, q, :, 0:cols] = block[q * channels : (q + 1) * channels, :]
        tail = pltpu.roll(packed, (LANES - 2 * RIM * q - RIM) % LANES, 1)
        work[0, q, :, cols:width] = jnp.where((lane < RIM) | (lane >= LANES - RIM), tail, 0.0)
    base = base + half
    start = 0 if low else keep
    stage[start : start + SWEEPS, 0:cols] = block[base : base + SWEEPS, :]
    stage[start : start + SWEEPS, cols:width] = block[base + 8 : base + 8 + SWEEPS, 0:LANES]
    if low:
        stage[SWEEPS:rows, :] = coef[0:keep, :]
    else:
        stage[0:keep, :] = coef[SWEEPS:rows, :]
    set_faces(faces, stage[...])

    def loader(t):
        def load(r, g):
            j = r + 1 if low else r - 1
            if 0 <= j < SWEEPS:
                return work[t % 2, j, part(g), :]
            return edge[t, j - SWEEPS if low else r + 1, part(g), :]

        return load

    def storer(t):
        def store(r, g, values):
            work[(t + 1) % 2, r, part(g), :] = values

        return store

    for t in range(SWEEPS):
        load = loader(t)
        swept(load, turns(load, SWEEPS, width), faces, t + 1 if low else keep - 1 - t, storer(t))

    for i in range(0 if low else rows // 2, rows // 2 if low else rows):
        if SWEEPS <= i < keep:
            done = middle[i - SWEEPS, :, 0:cols]
        else:
            done = work[SWEEPS % 2, i if low else i - keep, :, 0:cols]
        done = done * spread[i]
        for k in range(cols // LANES):
            first = k * 8 + i % 8
            result[pl.ds(first, channels, stride=rows // 2 * cols // LANES), :] = done[:, k * LANES : (k + 1) * LANES]
    size = rows // 2 * cols // LANES
    target = out.at[:, 0:size, :] if low else out.at[:, size : 2 * size, :]
    copy = pltpu.make_async_copy(result.reshape(channels, size, LANES), target, sent)
    copy.start()
    copy.wait()


def per_device(
    obs_innovation,
    obs_precision,
    obs_offsets,
    obs_cell,
    obs_counts,
    land_sea,
    diffusivity,
    background_std,
):
    dests, slots = obs_innovation.shape[2:]
    channels, rows, cols = background_std.shape
    width = cols + LANES
    count_rows, count_cols = lax.axis_size("row"), lax.axis_size("col")
    records = dests * slots

    by_slot = lambda x: x.reshape(dests, slots).T
    offsets = obs_offsets.reshape(dests, 2, slots).transpose(1, 2, 0)
    vmem = lambda *shape: pltpu.VMEM(shape, jnp.float32)
    bf16 = lambda *shape: pltpu.VMEM(shape, jnp.bfloat16)
    packed = kernel_call(
        pack_body,
        "pack_records",
        f32(dests, 1, 3 * LANES),
        (by_slot(obs_innovation), by_slot(obs_precision), offsets, by_slot(obs_cell), obs_counts.reshape(1, dests)),
        [
            vmem(slots, dests),
            vmem(slots, dests),
            vmem(2, slots, dests),
            pltpu.VMEM((slots, dests), jnp.int32),
            pltpu.VMEM((1, dests), jnp.int32),
            vmem(LANES, LANES),
            vmem(LANES, LANES),
            pltpu.SemaphoreType.DMA((5,)),
        ],
        moved=200_000,
        place=pltpu.HBM,
        grant=ALL_VMEM_BYTES,
    )
    arrived = lax.all_to_all(packed, "col", split_axis=0, concat_axis=0, tiled=True, axis_index_groups=[list(range(dests))[::-1]])

    spread, coef, near, far = kernel_call(
        fixed_body,
        "fixed_fields",
        (f32(rows, channels, cols), f32(rows, cols), f32(channels + 8, LANES), f32(channels + 8, LANES)),
        (background_std, land_sea, diffusivity),
        [vmem(cols // LANES, channels * rows, LANES)],
        moved=2_000_000,
    )
    near = lax.ppermute(near, "col", [(i, i ^ 1) for i in range(count_cols)])
    far = lax.ppermute(far, "col", [(i, (((i + 1) ^ 1) - 1) % count_cols) for i in range(count_cols)])

    blocks = records // LANES
    chunks = min(CHUNKS, blocks)
    piece = records // chunks
    state, sides = kernel_call(
        build_body,
        "build_state",
        (f32(rows, channels, cols), f32(2, channels, LANES)),
        (arrived, spread),
        [pltpu.VMEM((3, 3, blocks, LANES), jnp.int32), vmem(3, 10, blocks, LANES), vmem(rows * channels, cols)]
        + [bf16(rows * channels, piece)] * (2 * chunks)
        + [bf16(cols, piece)] * (2 * chunks)
        + [bf16(2, 2 * channels, piece)] * chunks
        + [bf16(2, rows * RIM, piece)] * (2 * chunks),
        moved=10_000_000,
    )
    slab = SWEEPS * channels + channels // 2 + 16
    tails, coef_wide, to_up, to_down = kernel_call(
        rim_body,
        "build_rims",
        (f32(rows, channels, LANES), f32(rows, width), f32(slab, cols), f32(slab, cols)),
        (state, sides, coef, near, far),
        moved=2_000_000,
    )
    up = [(i, i + 1) for i in range(count_rows - 1)]
    down = [(j, i) for i, j in up]
    from_down = lax.ppermute(to_up, "row", up)
    from_up = lax.ppermute(to_down, "row", down)

    edge_low, edge_high, middle = kernel_call(
        inner_body,
        "inner_sweeps",
        (
            f32(SWEEPS, 2, channels, width),
            f32(SWEEPS, 2, channels, width),
            f32(rows - 2 * SWEEPS, channels, width),
        ),
        (state, tails, coef_wide),
        [vmem(2, rows, channels, width), vmem(5, rows, width)],
        moved=6_000_000,
    )
    size = rows * cols // LANES
    out = None
    for low, edge, block in ((True, edge_low, from_down), (False, edge_high, from_up)):
        out = kernel_call(
            functools.partial(side_body, low),
            "low_sweeps" if low else "high_sweeps",
            f32(channels, size, LANES),
            (edge, middle, coef_wide, spread, block) + (() if low else (out,)),
            [
                vmem(2, SWEEPS, channels, width),
                vmem(5, rows, width),
                vmem(rows, width),
                vmem(channels * size // 2, LANES),
                pltpu.SemaphoreType.DMA,
            ],
            moved=5_000_000,
            held=() if low else (5,),
            out_place=pltpu.HBM,
        )
    out = out.reshape(channels, rows // 8, cols // LANES, 8, LANES)
    return out.transpose(0, 1, 3, 2, 4).reshape(channels, rows, cols)


def solution(mesh):
    placed = (
        P("row", "col", None, None),
        P("row", "col", None, None),
        P("row", "col", None, None, None),
        P("row", "col", None, None),
        P("row", "col", None),
        P("row", "col"),
        P("row", "col"),
        P(None, "row", "col"),
    )
    return jax.shard_map(
        per_device, mesh=mesh, in_specs=placed, out_specs=P(None, "row", "col"), check_vma=False
    )
```

```python
import functools

import jax
import jax.numpy as jnp
from jax import lax
from jax.experimental import pallas as pl
from jax.experimental.pallas import tpu as pltpu
from jax.sharding import PartitionSpec as P

SWEEPS = 6
LANES = 128
CHUNKS = 4
RIM = 8
VMEM_BYTES = 24 * 1024 * 1024
ALL_VMEM_BYTES = 58 * 1024 * 1024

NT = (((1,), (1,)), ((), ()))


def kernel_call(body, name, outs, inputs, scratch=(), moved=0, place=pltpu.VMEM, grant=VMEM_BYTES, held=(), out_place=pltpu.VMEM):
    specs = [pl.BlockSpec(memory_space=out_place if k in held else place) for k in range(len(inputs))]
    return pl.pallas_call(
        body,
        name=name,
        out_shape=outs,
        in_specs=specs,
        out_specs=jax.tree.map(lambda _: pl.BlockSpec(memory_space=out_place), outs),
        scratch_shapes=list(scratch),
        input_output_aliases={k: 0 for k in held},
        compiler_params=pltpu.CompilerParams(vmem_limit_bytes=grant),
        cost_estimate=pl.CostEstimate(flops=0, bytes_accessed=moved, transcendentals=0),
    )(*inputs)


def f32(*shape):
    return jax.ShapeDtypeStruct(shape, jnp.float32)


def pack_body(innovation_in, precision_in, offsets_in, cells_in, counts_in, out, innovation, precision, offsets, cells, counts, tile, rows, arrived):
    pairs = (
        (counts_in, counts),
        (innovation_in, innovation),
        (precision_in, precision),
        (offsets_in, offsets),
        (cells_in, cells),
    )
    copies = [pltpu.make_async_copy(source, held, arrived.at[k]) for k, (source, held) in enumerate(pairs)]
    for copy in copies:
        copy.start()
    for copy in copies:
        copy.wait()
    slots, dests = innovation.shape
    live = lax.broadcasted_iota(jnp.int32, (slots, dests), 0) < counts[...]
    tile[0:slots, 0:dests] = jnp.where(live, innovation[...] * precision[...], 0.0)
    tile[slots : 2 * slots, 0:dests] = offsets[0]
    tile[2 * slots : 3 * slots, 0:dests] = offsets[1]
    tile[3 * slots : 4 * slots, 0:dests] = cells[...].astype(jnp.float32)
    rows[...] = tile[...].T
    for d in range(dests):
        for k in range(3):
            out[dests - 1 - d, :, k * LANES : (k + 1) * LANES] = rows[pl.ds((d + k - 1) % dests, 1), :]


def odd_column():
    return lax.rem(lax.axis_index("col"), 2) == 1


def fixed_body(std, sea, diffusivity, spread, coef, far, near, stage):
    channels, rows, cols = std.shape
    mask = sea[...].astype(jnp.float32)
    product = std[...].astype(jnp.float32) * mask[None]
    for part in range(cols // LANES):
        stage[part] = product[:, :, part * LANES : (part + 1) * LANES].reshape(channels * rows, LANES)
    coef[...] = diffusivity[...] * mask
    lane = lax.broadcasted_iota(jnp.int32, (channels, LANES), 1)
    ends = [jnp.zeros((channels, LANES), jnp.float32)] * 2
    for i in range(rows):
        here = [stage[part, pl.ds(i, channels, stride=rows), :] for part in range(cols // LANES)]
        for part, values in enumerate(here):
            spread[i, :, part * LANES : (part + 1) * LANES] = values
        inside = (lane >= RIM * i) & (lane < RIM * (i + 1))
        ends[0] = jnp.where(inside, pltpu.roll(here[0], (RIM * i) % LANES, 1), ends[0])
        ends[1] = jnp.where(inside, pltpu.roll(here[-1], (RIM * i + RIM) % LANES, 1), ends[1])
    lane_row = lax.broadcasted_iota(jnp.int32, (1, LANES), 1)
    for which in range(2):
        edge = coef[:, 0:LANES] if which == 0 else coef[:, cols - LANES : cols]
        packed = jnp.zeros((1, LANES), jnp.float32)
        for i in range(rows):
            inside = (lane_row >= RIM * i) & (lane_row < RIM * (i + 1))
            turned = pltpu.roll(edge[i : i + 1], (RIM * i + RIM * which) % LANES, 1)
            packed = jnp.where(inside, turned, packed)
        ends[which] = jnp.concatenate([ends[which], jnp.broadcast_to(packed, (8, LANES))], axis=0)
    odd = odd_column()
    near[...] = jnp.where(odd, ends[0], ends[1])
    far[...] = jnp.where(odd, ends[1], ends[0])


def record_fields(block, slots):
    quarter = block.shape[0] // 4
    lane = lax.broadcasted_iota(jnp.int32, (quarter, LANES), 1)
    fields = []
    for f in range(4):
        joined = None
        for b in range(4):
            part = block[b * quarter : (b + 1) * quarter]
            turn = (slots * (b - f)) % LANES
            if turn:
                part = pltpu.roll(part, turn, 1)
            joined = part if b == 0 else jnp.where(lane >= slots * b, part, joined)
        fields.append(joined)
    return fields


def build_body(arrived, spread, state, sides, whole, real, total, *held):
    rows, channels, cols = spread.shape
    slots = LANES // 4
    blocks = whole.shape[2]
    chunks = len(held) // 7
    a_high, a_low, b_high, b_low, c_both, d_high, d_low = [held[q * chunks : (q + 1) * chunks] for q in range(7)]

    for k in range(3):
        weight, east, north, cell = record_fields(arrived[:, 0, k * LANES : (k + 1) * LANES], slots)
        cell = cell.astype(jnp.int32)
        for f, values in enumerate((cell >> 12, (cell >> 8) & 15, cell & 255)):
            whole[k, f] = values
        if k == 1:
            parts = (weight * (1.0 - north), weight * north, 1.0 - east, east)
        else:
            parts = (1.0 - north, north, 1.0 - east, east, weight)
        for f, values in enumerate(parts):
            high = values.astype(jnp.bfloat16).astype(jnp.float32)
            if k == 1 or f == 4:
                real[k, 2 * f] = high
                real[k, 2 * f + 1] = values - high
            else:
                real[k, 2 * f] = values

    def pick(away, at, after):
        return jnp.where(away == 0, at, jnp.where(away == 1, after, 0.0))

    def block(n, c, here):
        row_of = lambda k, f: real[k, f, n : n + 1, :]
        index = lambda k, f, size: lax.broadcasted_iota(jnp.int32, (size, LANES), 0) - whole[k, f, n : n + 1, :]

        hot = jnp.where(index(1, 0, channels) == 0, 1.0, 0.0).astype(jnp.bfloat16)
        away = index(1, 1, rows)
        high, low = pick(away, row_of(1, 0), row_of(1, 2)), pick(away, row_of(1, 1), row_of(1, 3))
        wide = lambda x: jnp.broadcast_to(x, (channels, LANES)).astype(jnp.bfloat16)
        for row in range(rows):
            at = slice(row * channels, (row + 1) * channels)
            a_high[c][at, here] = hot * wide(high[row : row + 1])
            a_low[c][at, here] = hot * wide(low[row : row + 1])
        tile = lambda x: jnp.broadcast_to(x, (16, LANES)).astype(jnp.bfloat16)
        column = whole[1, 2, n : n + 1, :].astype(jnp.float32)
        at, after = tile(column), tile(column + 1.0)
        factors = [tile(row_of(1, f)) for f in (4, 5, 6, 7)]
        none = jnp.zeros((16, LANES), jnp.bfloat16)
        for q in range(cols // 16):
            some = slice(16 * q, 16 * (q + 1))
            line = (lax.broadcasted_iota(jnp.int32, (16, LANES), 0) + 16 * q).astype(jnp.float32).astype(jnp.bfloat16)
            first, second = line == at, line == after
            b_high[c][some, here] = jnp.where(first, factors[0], jnp.where(second, factors[2], none))
            b_low[c][some, here] = jnp.where(first, factors[1], jnp.where(second, factors[3], none))

        for side, (k, base) in enumerate(((0, cols - RIM), (2, 0))):
            hot = index(k, 0, channels) == 0
            for part in range(2):
                at = slice(part * channels, (part + 1) * channels)
                c_both[c][side, at, here] = jnp.where(hot, row_of(k, 8 + part), 0.0).astype(jnp.bfloat16)
            by_row = pick(index(k, 1, rows), row_of(k, 0), row_of(k, 2))
            by_col = pick(index(k, 2, RIM) + base, row_of(k, 4), row_of(k, 6))
            both = (by_row[:, None, :] * by_col[None, :, :]).reshape(rows * RIM, LANES)
            high = both.astype(jnp.bfloat16)
            d_high[c][side, :, here] = high
            d_low[c][side, :, here] = (both - high.astype(jnp.float32)).astype(jnp.bfloat16)

    dot = lambda x, y: lax.dot_general(x, y, NT, preferred_element_type=jnp.float32)
    per = blocks // chunks
    rim = [0.0, 0.0]
    for c in range(chunks):
        for n in range(per):
            block(c * per + n, c, slice(n * LANES, (n + 1) * LANES))
        first, second = b_high[c][...], b_low[c][...]
        part = dot(a_high[c][...], first) + (dot(a_high[c][...], second) + dot(a_low[c][...], first))
        total[...] = part if c == 0 else total[...] + part
        for side in range(2):
            first = dot(c_both[c][side], d_high[c][side])
            second = dot(c_both[c][side, 0:channels], d_low[c][side])
            rim[side] = rim[side] + (first[0:channels] + (first[channels:] + second))
    for side in range(2):
        sides[side] = rim[side]
    for i in range(rows):
        state[i] = total[i * channels : (i + 1) * channels, :] * spread[i]


def rim_body(state, sides, coef, far, near, tails, coef_out, to_up, to_down):
    rows, channels, cols = state.shape
    lane = lax.broadcasted_iota(jnp.int32, (channels, LANES), 1)
    lane_row = lax.broadcasted_iota(jnp.int32, (1, LANES), 1)

    def outer(left, right, i, lanes):
        left = pltpu.roll(left, (LANES - RIM - RIM * i) % LANES, 1)
        right = pltpu.roll(right, (LANES - RIM * i) % LANES, 1)
        return jnp.where(lanes < RIM, right, jnp.where(lanes >= LANES - RIM, left, 0.0))

    odd = odd_column()
    rim_left = jnp.where(odd, near[...], far[...])
    rim_right = jnp.where(odd, far[...], near[...])
    left = sides[0] * rim_left[0:channels]
    right = sides[1] * rim_right[0:channels]
    coef_out[:, 0:cols] = coef[...]
    for i in range(rows):
        tails[i] = outer(left, right, i, lane)
        coef_out[i : i + 1, cols : cols + LANES] = outer(
            rim_left[channels : channels + 1], rim_right[channels : channels + 1], i, lane_row
        )

    for out, start in ((to_down, 0), (to_up, rows - SWEEPS)):
        packed = jnp.zeros((channels, LANES), jnp.float32)
        for q in range(SWEEPS):
            i = start + q
            out[q * channels : (q + 1) * channels, :] = state[i]
            inside = (lane >= 2 * RIM * q) & (lane < 2 * RIM * (q + 1))
            packed = jnp.where(inside, pltpu.roll(tails[i], (2 * RIM * q + RIM) % LANES, 1), packed)
        base = SWEEPS * channels
        half = channels // 2
        out[base : base + half, 0:LANES] = packed[0:half]
        out[base : base + half, LANES : 2 * LANES] = packed[half:channels]
        base = base + half
        out[base : base + 8, :] = jnp.zeros((8, cols), jnp.float32)
        out[base : base + SWEEPS, :] = coef_out[start : start + SWEEPS, 0:cols]
        out[base + 8 : base + 16, :] = jnp.zeros((8, cols), jnp.float32)
        out[base + 8 : base + 8 + SWEEPS, 0:LANES] = coef_out[start : start + SWEEPS, cols : cols + LANES]


def set_faces(faces, field):
    rows, width = field.shape
    east = jnp.sqrt(field * pltpu.roll(field, width - 1, 1))
    north = jnp.sqrt(field * pltpu.roll(field, rows - 1, 0))
    west = pltpu.roll(east, 1, 1)
    south = pltpu.roll(north, 1, 0)
    faces[0, 0:rows] = 1.0 - ((east + west) + (north + south))
    for k, values in enumerate((east, west, north, south)):
        faces[1 + k, 0:rows] = values


def turns(load, count, width):
    return [[(pltpu.roll(load(r, g), width - 1, 1), pltpu.roll(load(r, g), 1, 1)) for r in range(count)] for g in range(4)]


def swept(load, turned, faces, first, store):
    width = faces.shape[2]
    for r in range(len(turned[0])):
        c, e, w, n, s = [jnp.broadcast_to(faces[k, pl.ds(first + r, 1), :], (8, width)) for k in range(5)]
        for g in range(len(turned)):
            east, west = turned[g][r]
            store(r, g, (c * load(r, g) + (e * east + w * west)) + (n * load(r + 1, g) + s * load(r - 1, g)))


def side_by_side(state, tails, i, g):
    here = slice(8 * g, 8 * (g + 1))
    return jnp.concatenate([state[i, here, :], tails[i, here, :]], axis=1)


def inner_body(state, tails, coef, edge_low, edge_high, middle, work, faces):
    rows, channels, cols = state.shape
    width = cols + LANES
    part = lambda g: slice(8 * g, 8 * (g + 1))

    set_faces(faces, coef[...])
    for g in range(channels // 8):
        for k in range(2):
            edge_low[0, k, part(g), :] = side_by_side(state, tails, k, g)
            edge_high[0, k, part(g), :] = side_by_side(state, tails, rows - 2 + k, g)

    def loader(t):
        if t == 0:
            return lambda r, g: side_by_side(state, tails, 1 + r, g)
        return lambda r, g: work[t % 2, t + 1 + r, part(g), :]

    def storer(t):
        def store(r, g, values):
            done, row = t + 1, t + 1 + r
            if done == SWEEPS:
                middle[r, part(g), :] = values
                return
            work[done % 2, row, part(g), :] = values
            if row < done + 2:
                edge_low[done, row - done, part(g), :] = values
            if row >= rows - 2 - done:
                edge_high[done, row - (rows - 2 - done), part(g), :] = values

        return store

    for t in range(SWEEPS):
        load, count = loader(t), rows - 2 * (t + 1)
        swept(load, turns(load, count, width), faces, t + 1, storer(t))


def side_body(low, edge, middle, coef, spread, block, *rest):
    out, work, faces, stage, result, sent = rest[-6:]
    rows, channels, cols = spread.shape
    width = cols + LANES
    half = channels // 2
    keep = rows - SWEEPS
    lane = lax.broadcasted_iota(jnp.int32, (channels, LANES), 1)
    part = lambda g: slice(8 * g, 8 * (g + 1))

    base = SWEEPS * channels
    packed = jnp.concatenate([block[base : base + half, 0:LANES], block[base : base + half, LANES : 2 * LANES]], axis=0)
    for q in range(SWEEPS):
        work[0, q, :, 0:cols] = block[q * channels : (q + 1) * channels, :]
        tail = pltpu.roll(packed, (LANES - 2 * RIM * q - RIM) % LANES, 1)
        work[0, q, :, cols:width] = jnp.where((lane < RIM) | (lane >= LANES - RIM), tail, 0.0)
    base = base + half
    start = 0 if low else keep
    stage[start : start + SWEEPS, 0:cols] = block[base : base + SWEEPS, :]
    stage[start : start + SWEEPS, cols:width] = block[base + 8 : base + 8 + SWEEPS, 0:LANES]
    if low:
        stage[SWEEPS:rows, :] = coef[0:keep, :]
    else:
        stage[0:keep, :] = coef[SWEEPS:rows, :]
    set_faces(faces, stage[...])

    def loader(t):
        def load(r, g):
            j = r + 1 if low else r - 1
            if 0 <= j < SWEEPS:
                return work[t % 2, j, part(g), :]
            return edge[t, j - SWEEPS if low else r + 1, part(g), :]

        return load

    def storer(t):
        def store(r, g, values):
            work[(t + 1) % 2, r, part(g), :] = values

        return store

    for t in range(SWEEPS):
        load = loader(t)
        swept(load, turns(load, SWEEPS, width), faces, t + 1 if low else keep - 1 - t, storer(t))

    size = rows // 2 * cols // LANES
    target = out.at[:, 0:size, :] if low else out.at[:, size : 2 * size, :]
    source = result.reshape(channels, size, LANES)
    copies = []
    for g in range(channels // 8):
        for i in range(0 if low else rows // 2, rows // 2 if low else rows):
            if SWEEPS <= i < keep:
                done = middle[i - SWEEPS, part(g), 0:cols]
            else:
                done = work[SWEEPS % 2, i if low else i - keep, part(g), 0:cols]
            done = done * spread[i, part(g), :]
            for k in range(cols // LANES):
                first = 8 * g * size + k * 8 + i % 8
                result[pl.ds(first, 8, stride=size), :] = done[:, k * LANES : (k + 1) * LANES]
        copies.append(pltpu.make_async_copy(source.at[part(g)], target.at[part(g)], sent.at[g]))
        copies[-1].start()
    for copy in copies:
        copy.wait()


def per_device(
    obs_innovation,
    obs_precision,
    obs_offsets,
    obs_cell,
    obs_counts,
    land_sea,
    diffusivity,
    background_std,
):
    dests, slots = obs_innovation.shape[2:]
    channels, rows, cols = background_std.shape
    width = cols + LANES
    count_rows, count_cols = lax.axis_size("row"), lax.axis_size("col")
    records = dests * slots

    by_slot = lambda x: x.reshape(dests, slots).T
    offsets = obs_offsets.reshape(dests, 2, slots).transpose(1, 2, 0)
    vmem = lambda *shape: pltpu.VMEM(shape, jnp.float32)
    bf16 = lambda *shape: pltpu.VMEM(shape, jnp.bfloat16)
    packed = kernel_call(
        pack_body,
        "pack_records",
        f32(dests, 1, 3 * LANES),
        (by_slot(obs_innovation), by_slot(obs_precision), offsets, by_slot(obs_cell), obs_counts.reshape(1, dests)),
        [
            vmem(slots, dests),
            vmem(slots, dests),
            vmem(2, slots, dests),
            pltpu.VMEM((slots, dests), jnp.int32),
            pltpu.VMEM((1, dests), jnp.int32),
            vmem(LANES, LANES),
            vmem(LANES, LANES),
            pltpu.SemaphoreType.DMA((5,)),
        ],
        moved=200_000,
        place=pltpu.HBM,
        grant=ALL_VMEM_BYTES,
    )
    arrived = lax.all_to_all(packed, "col", split_axis=0, concat_axis=0, tiled=True, axis_index_groups=[list(range(dests))[::-1]])

    spread, coef, far, near = kernel_call(
        fixed_body,
        "fixed_fields",
        (f32(rows, channels, cols), f32(rows, cols), f32(channels + 8, LANES), f32(channels + 8, LANES)),
        (background_std, land_sea, diffusivity),
        [vmem(cols // LANES, channels * rows, LANES)],
        moved=2_000_000,
    )
    far = lax.ppermute(far, "col", [(i, (((i + 1) ^ 1) - 1) % count_cols) for i in range(count_cols)])
    near = lax.ppermute(near, "col", [(i, i ^ 1) for i in range(count_cols)])

    blocks = records // LANES
    chunks = min(CHUNKS, blocks)
    piece = records // chunks
    state, sides = kernel_call(
        build_body,
        "build_state",
        (f32(rows, channels, cols), f32(2, channels, LANES)),
        (arrived, spread),
        [pltpu.VMEM((3, 3, blocks, LANES), jnp.int32), vmem(3, 10, blocks, LANES), vmem(rows * channels, cols)]
        + [bf16(rows * channels, piece)] * (2 * chunks)
        + [bf16(cols, piece)] * (2 * chunks)
        + [bf16(2, 2 * channels, piece)] * chunks
        + [bf16(2, rows * RIM, piece)] * (2 * chunks),
        moved=10_000_000,
    )
    slab = SWEEPS * channels + channels // 2 + 16
    tails, coef_wide, to_up, to_down = kernel_call(
        rim_body,
        "build_rims",
        (f32(rows, channels, LANES), f32(rows, width), f32(slab, cols), f32(slab, cols)),
        (state, sides, coef, far, near),
        moved=2_000_000,
    )
    up = [(i, i + 1) for i in range(count_rows - 1)]
    down = [(j, i) for i, j in up]
    from_down = lax.ppermute(to_up, "row", up)
    from_up = lax.ppermute(to_down, "row", down)

    edge_low, edge_high, middle = kernel_call(
        inner_body,
        "inner_sweeps",
        (
            f32(SWEEPS, 2, channels, width),
            f32(SWEEPS, 2, channels, width),
            f32(rows - 2 * SWEEPS, channels, width),
        ),
        (state, tails, coef_wide),
        [vmem(2, rows, channels, width), vmem(5, rows, width)],
        moved=6_000_000,
    )
    size = rows * cols // LANES
    out = None
    for low, edge, block in ((True, edge_low, from_down), (False, edge_high, from_up)):
        out = kernel_call(
            functools.partial(side_body, low),
            "low_sweeps" if low else "high_sweeps",
            f32(channels, size, LANES),
            (edge, middle, coef_wide, spread, block) + (() if low else (out,)),
            [
                vmem(2, SWEEPS, channels, width),
                vmem(5, rows, width),
                vmem(rows, width),
                vmem(channels * size // 2, LANES),
                pltpu.SemaphoreType.DMA((channels // 8,)),
            ],
            moved=5_000_000,
            held=() if low else (5,),
            out_place=pltpu.HBM,
        )
    out = out.reshape(channels, rows // 8, cols // LANES, 8, LANES)
    return out.transpose(0, 1, 3, 2, 4).reshape(channels, rows, cols)


def solution(mesh):
    placed = (
        P("row", "col", None, None),
        P("row", "col", None, None),
        P("row", "col", None, None, None),
        P("row", "col", None, None),
        P("row", "col", None),
        P("row", "col"),
        P("row", "col"),
        P(None, "row", "col"),
    )
    return jax.shard_map(
        per_device, mesh=mesh, in_specs=placed, out_specs=P(None, "row", "col"), check_vma=False
    )
```

```python
import functools

import jax
import jax.numpy as jnp
from jax import lax
from jax.experimental import pallas as pl
from jax.experimental.pallas import tpu as pltpu
from jax.sharding import PartitionSpec as P

SWEEPS = 6
LANES = 128
CHUNKS = 4
RIM = 8
VMEM_BYTES = 24 * 1024 * 1024
ALL_VMEM_BYTES = 58 * 1024 * 1024

NT = (((1,), (1,)), ((), ()))


def kernel_call(body, name, outs, inputs, scratch=(), moved=0, place=pltpu.VMEM, grant=VMEM_BYTES, held=(), out_place=pltpu.VMEM):
    specs = [pl.BlockSpec(memory_space=out_place if k in held else place) for k in range(len(inputs))]
    return pl.pallas_call(
        body,
        name=name,
        out_shape=outs,
        in_specs=specs,
        out_specs=jax.tree.map(lambda _: pl.BlockSpec(memory_space=out_place), outs),
        scratch_shapes=list(scratch),
        input_output_aliases={k: 0 for k in held},
        compiler_params=pltpu.CompilerParams(vmem_limit_bytes=grant),
        cost_estimate=pl.CostEstimate(flops=0, bytes_accessed=moved, transcendentals=0),
    )(*inputs)


def f32(*shape):
    return jax.ShapeDtypeStruct(shape, jnp.float32)


def pack_body(innovation_in, precision_in, offsets_in, cells_in, counts_in, out, innovation, precision, offsets, cells, counts, tile, rows, arrived):
    pairs = (
        (counts_in, counts),
        (innovation_in, innovation),
        (precision_in, precision),
        (offsets_in, offsets),
        (cells_in, cells),
    )
    copies = [pltpu.make_async_copy(source, held, arrived.at[k]) for k, (source, held) in enumerate(pairs)]
    for copy in copies:
        copy.start()
    for copy in copies:
        copy.wait()
    slots, dests = innovation.shape
    live = lax.broadcasted_iota(jnp.int32, (slots, dests), 0) < counts[...]
    tile[0:slots, 0:dests] = jnp.where(live, innovation[...] * precision[...], 0.0)
    tile[slots : 2 * slots, 0:dests] = offsets[0]
    tile[2 * slots : 3 * slots, 0:dests] = offsets[1]
    tile[3 * slots : 4 * slots, 0:dests] = cells[...].astype(jnp.float32)
    rows[...] = tile[...].T
    for d in range(dests):
        for k in range(3):
            out[dests - 1 - d, :, k * LANES : (k + 1) * LANES] = rows[pl.ds((d + k - 1) % dests, 1), :]


def odd_column():
    return lax.rem(lax.axis_index("col"), 2) == 1


def fixed_body(std, sea, diffusivity, spread, coef, far, near, stage):
    channels, rows, cols = std.shape
    mask = sea[...].astype(jnp.float32)
    product = std[...].astype(jnp.float32) * mask[None]
    for part in range(cols // LANES):
        stage[part] = product[:, :, part * LANES : (part + 1) * LANES].reshape(channels * rows, LANES)
    coef[...] = diffusivity[...] * mask
    lane = lax.broadcasted_iota(jnp.int32, (channels, LANES), 1)
    ends = [jnp.zeros((channels, LANES), jnp.float32)] * 2
    for i in range(rows):
        here = [stage[part, pl.ds(i, channels, stride=rows), :] for part in range(cols // LANES)]
        for part, values in enumerate(here):
            spread[i, :, part * LANES : (part + 1) * LANES] = values
        inside = (lane >= RIM * i) & (lane < RIM * (i + 1))
        ends[0] = jnp.where(inside, pltpu.roll(here[0], (RIM * i) % LANES, 1), ends[0])
        ends[1] = jnp.where(inside, pltpu.roll(here[-1], (RIM * i + RIM) % LANES, 1), ends[1])
    lane_row = lax.broadcasted_iota(jnp.int32, (1, LANES), 1)
    for which in range(2):
        edge = coef[:, 0:LANES] if which == 0 else coef[:, cols - LANES : cols]
        packed = jnp.zeros((1, LANES), jnp.float32)
        for i in range(rows):
            inside = (lane_row >= RIM * i) & (lane_row < RIM * (i + 1))
            turned = pltpu.roll(edge[i : i + 1], (RIM * i + RIM * which) % LANES, 1)
            packed = jnp.where(inside, turned, packed)
        ends[which] = jnp.concatenate([ends[which], jnp.broadcast_to(packed, (8, LANES))], axis=0)
    odd = odd_column()
    near[...] = jnp.where(odd, ends[0], ends[1])
    far[...] = jnp.where(odd, ends[1], ends[0])


def record_fields(block, slots):
    quarter = block.shape[0] // 4
    lane = lax.broadcasted_iota(jnp.int32, (quarter, LANES), 1)
    fields = []
    for f in range(4):
        joined = None
        for b in range(4):
            part = block[b * quarter : (b + 1) * quarter]
            turn = (slots * (b - f)) % LANES
            if turn:
                part = pltpu.roll(part, turn, 1)
            joined = part if b == 0 else jnp.where(lane >= slots * b, part, joined)
        fields.append(joined)
    return fields


def build_body(arrived, spread, state, sides, whole, real, total, *held):
    rows, channels, cols = spread.shape
    slots = LANES // 4
    blocks = whole.shape[2]
    chunks = len(held) // 7
    a_high, a_low, b_high, b_low, c_both, d_high, d_low = [held[q * chunks : (q + 1) * chunks] for q in range(7)]

    for k in range(3):
        weight, east, north, cell = record_fields(arrived[:, 0, k * LANES : (k + 1) * LANES], slots)
        cell = cell.astype(jnp.int32)
        for f, values in enumerate((cell >> 12, (cell >> 8) & 15, cell & 255)):
            whole[k, f] = values
        if k == 1:
            parts = (weight * (1.0 - north), weight * north, 1.0 - east, east)
        else:
            parts = (1.0 - north, north, 1.0 - east, east, weight)
        for f, values in enumerate(parts):
            high = values.astype(jnp.bfloat16).astype(jnp.float32)
            if k == 1 or f == 4:
                real[k, 2 * f] = high
                real[k, 2 * f + 1] = values - high
            else:
                real[k, 2 * f] = values

    def pick(away, at, after):
        return jnp.where(away == 0, at, jnp.where(away == 1, after, 0.0))

    def block(n, c, here):
        row_of = lambda k, f: real[k, f, n : n + 1, :]
        index = lambda k, f, size: lax.broadcasted_iota(jnp.int32, (size, LANES), 0) - whole[k, f, n : n + 1, :]

        hot = jnp.where(index(1, 0, channels) == 0, 1.0, 0.0).astype(jnp.bfloat16)
        away = index(1, 1, rows)
        high, low = pick(away, row_of(1, 0), row_of(1, 2)), pick(away, row_of(1, 1), row_of(1, 3))
        wide = lambda x: jnp.broadcast_to(x, (channels, LANES)).astype(jnp.bfloat16)
        for row in range(rows):
            at = slice(row * channels, (row + 1) * channels)
            a_high[c][at, here] = hot * wide(high[row : row + 1])
            a_low[c][at, here] = hot * wide(low[row : row + 1])
        tile = lambda x: jnp.broadcast_to(x, (16, LANES)).astype(jnp.bfloat16)
        column = whole[1, 2, n : n + 1, :].astype(jnp.float32)
        at, after = tile(column), tile(column + 1.0)
        factors = [tile(row_of(1, f)) for f in (4, 5, 6, 7)]
        none = jnp.zeros((16, LANES), jnp.bfloat16)
        for q in range(cols // 16):
            some = slice(16 * q, 16 * (q + 1))
            line = (lax.broadcasted_iota(jnp.int32, (16, LANES), 0) + 16 * q).astype(jnp.float32).astype(jnp.bfloat16)
            first, second = line == at, line == after
            b_high[c][some, here] = jnp.where(first, factors[0], jnp.where(second, factors[2], none))
            b_low[c][some, here] = jnp.where(first, factors[1], jnp.where(second, factors[3], none))

        for side, (k, base) in enumerate(((0, cols - RIM), (2, 0))):
            hot = index(k, 0, channels) == 0
            for part in range(2):
                at = slice(part * channels, (part + 1) * channels)
                c_both[c][side, at, here] = jnp.where(hot, row_of(k, 8 + part), 0.0).astype(jnp.bfloat16)
            by_row = pick(index(k, 1, rows), row_of(k, 0), row_of(k, 2))
            by_col = pick(index(k, 2, RIM) + base, row_of(k, 4), row_of(k, 6))
            both = (by_row[:, None, :] * by_col[None, :, :]).reshape(rows * RIM, LANES)
            high = both.astype(jnp.bfloat16)
            d_high[c][side, :, here] = high
            d_low[c][side, :, here] = (both - high.astype(jnp.float32)).astype(jnp.bfloat16)

    dot = lambda x, y: lax.dot_general(x, y, NT, preferred_element_type=jnp.float32)
    per = blocks // chunks
    rim = [0.0, 0.0]
    for c in range(chunks):
        for n in range(per):
            block(c * per + n, c, slice(n * LANES, (n + 1) * LANES))
        first, second = b_high[c][...], b_low[c][...]
        part = dot(a_high[c][...], first) + (dot(a_high[c][...], second) + dot(a_low[c][...], first))
        total[...] = part if c == 0 else total[...] + part
        for side in range(2):
            first = dot(c_both[c][side], d_high[c][side])
            second = dot(c_both[c][side, 0:channels], d_low[c][side])
            rim[side] = rim[side] + (first[0:channels] + (first[channels:] + second))
    for side in range(2):
        sides[side] = rim[side]
    for i in range(rows):
        state[i] = total[i * channels : (i + 1) * channels, :] * spread[i]


def rim_body(state, sides, coef, far, near, tails, coef_out, to_up, to_down):
    rows, channels, cols = state.shape
    lane = lax.broadcasted_iota(jnp.int32, (channels, LANES), 1)
    lane_row = lax.broadcasted_iota(jnp.int32, (1, LANES), 1)

    def outer(left, right, i, lanes):
        left = pltpu.roll(left, (LANES - RIM - RIM * i) % LANES, 1)
        right = pltpu.roll(right, (LANES - RIM * i) % LANES, 1)
        return jnp.where(lanes < RIM, right, jnp.where(lanes >= LANES - RIM, left, 0.0))

    odd = odd_column()
    rim_left = jnp.where(odd, near[...], far[...])
    rim_right = jnp.where(odd, far[...], near[...])
    left = sides[0] * rim_left[0:channels]
    right = sides[1] * rim_right[0:channels]
    coef_out[:, 0:cols] = coef[...]
    for i in range(rows):
        tails[i] = outer(left, right, i, lane)
        coef_out[i : i + 1, cols : cols + LANES] = outer(
            rim_left[channels : channels + 1], rim_right[channels : channels + 1], i, lane_row
        )

    for out, start in ((to_down, 0), (to_up, rows - SWEEPS)):
        packed = jnp.zeros((channels, LANES), jnp.float32)
        for q in range(SWEEPS):
            i = start + q
            out[q * channels : (q + 1) * channels, :] = state[i]
            inside = (lane >= 2 * RIM * q) & (lane < 2 * RIM * (q + 1))
            packed = jnp.where(inside, pltpu.roll(tails[i], (2 * RIM * q + RIM) % LANES, 1), packed)
        base = SWEEPS * channels
        half = channels // 2
        out[base : base + half, 0:LANES] = packed[0:half]
        out[base : base + half, LANES : 2 * LANES] = packed[half:channels]
        base = base + half
        out[base : base + 8, :] = jnp.zeros((8, cols), jnp.float32)
        out[base : base + SWEEPS, :] = coef_out[start : start + SWEEPS, 0:cols]
        packed = jnp.zeros((1, LANES), jnp.float32)
        for q in range(SWEEPS):
            inside = (lane_row >= 2 * RIM * q) & (lane_row < 2 * RIM * (q + 1))
            tail = coef_out[start + q : start + q + 1, cols : cols + LANES]
            packed = jnp.where(inside, pltpu.roll(tail, (2 * RIM * q + RIM) % LANES, 1), packed)
        out[base + SWEEPS : base + SWEEPS + 1, 0:LANES] = packed


def set_faces(faces, field):
    rows, width = field.shape
    east = jnp.sqrt(field * pltpu.roll(field, width - 1, 1))
    north = jnp.sqrt(field * pltpu.roll(field, rows - 1, 0))
    west = pltpu.roll(east, 1, 1)
    south = pltpu.roll(north, 1, 0)
    faces[0, 0:rows] = 1.0 - ((east + west) + (north + south))
    for k, values in enumerate((east, west, north, south)):
        faces[1 + k, 0:rows] = values


def turns(load, count, width):
    return [[(pltpu.roll(load(r, g), width - 1, 1), pltpu.roll(load(r, g), 1, 1)) for r in range(count)] for g in range(4)]


def swept(load, turned, faces, first, store):
    width = faces.shape[2]
    for r in range(len(turned[0])):
        c, e, w, n, s = [jnp.broadcast_to(faces[k, pl.ds(first + r, 1), :], (8, width)) for k in range(5)]
        for g in range(len(turned)):
            east, west = turned[g][r]
            store(r, g, (c * load(r, g) + (e * east + w * west)) + (n * load(r + 1, g) + s * load(r - 1, g)))


def side_by_side(state, tails, i, g):
    here = slice(8 * g, 8 * (g + 1))
    return jnp.concatenate([state[i, here, :], tails[i, here, :]], axis=1)


def inner_body(state, tails, coef, edge_low, edge_high, middle, work, faces):
    rows, channels, cols = state.shape
    width = cols + LANES
    part = lambda g: slice(8 * g, 8 * (g + 1))

    set_faces(faces, coef[...])
    for g in range(channels // 8):
        for k in range(2):
            edge_low[0, k, part(g), :] = side_by_side(state, tails, k, g)
            edge_high[0, k, part(g), :] = side_by_side(state, tails, rows - 2 + k, g)

    def loader(t):
        if t == 0:
            return lambda r, g: side_by_side(state, tails, 1 + r, g)
        return lambda r, g: work[t % 2, t + 1 + r, part(g), :]

    def storer(t):
        def store(r, g, values):
            done, row = t + 1, t + 1 + r
            if done == SWEEPS:
                middle[r, part(g), :] = values
                return
            work[done % 2, row, part(g), :] = values
            if row < done + 2:
                edge_low[done, row - done, part(g), :] = values
            if row >= rows - 2 - done:
                edge_high[done, row - (rows - 2 - done), part(g), :] = values

        return store

    for t in range(SWEEPS):
        load, count = loader(t), rows - 2 * (t + 1)
        swept(load, turns(load, count, width), faces, t + 1, storer(t))


def side_body(low, edge, middle, coef, spread, block, *rest):
    out, work, faces, stage, result, sent = rest[-6:]
    rows, channels, cols = spread.shape
    width = cols + LANES
    half = channels // 2
    keep = rows - SWEEPS
    lane = lax.broadcasted_iota(jnp.int32, (channels, LANES), 1)
    part = lambda g: slice(8 * g, 8 * (g + 1))

    base = SWEEPS * channels
    packed = jnp.concatenate([block[base : base + half, 0:LANES], block[base : base + half, LANES : 2 * LANES]], axis=0)
    for q in range(SWEEPS):
        work[0, q, :, 0:cols] = block[q * channels : (q + 1) * channels, :]
        tail = pltpu.roll(packed, (LANES - 2 * RIM * q - RIM) % LANES, 1)
        work[0, q, :, cols:width] = jnp.where((lane < RIM) | (lane >= LANES - RIM), tail, 0.0)
    base = base + half
    start = 0 if low else keep
    stage[start : start + SWEEPS, 0:cols] = block[base : base + SWEEPS, :]
    packed = block[base + SWEEPS : base + SWEEPS + 1, 0:LANES]
    for q in range(SWEEPS):
        tail = pltpu.roll(packed, (LANES - 2 * RIM * q - RIM) % LANES, 1)
        stage[start + q : start + q + 1, cols:width] = jnp.where((lane[0:1] < RIM) | (lane[0:1] >= LANES - RIM), tail, 0.0)
    if low:
        stage[SWEEPS:rows, :] = coef[0:keep, :]
    else:
        stage[0:keep, :] = coef[SWEEPS:rows, :]
    set_faces(faces, stage[...])

    def loader(t):
        def load(r, g):
            j = r + 1 if low else r - 1
            if 0 <= j < SWEEPS:
                return work[t % 2, j, part(g), :]
            return edge[t, j - SWEEPS if low else r + 1, part(g), :]

        return load

    def storer(t):
        def store(r, g, values):
            work[(t + 1) % 2, r, part(g), :] = values

        return store

    for t in range(SWEEPS):
        load = loader(t)
        swept(load, turns(load, SWEEPS, width), faces, t + 1 if low else keep - 1 - t, storer(t))

    size = rows // 2 * cols // LANES
    target = out.at[:, 0:size, :] if low else out.at[:, size : 2 * size, :]
    source = result.reshape(channels, size, LANES)
    copies = []
    for g in range(channels // 8):
        for i in range(0 if low else rows // 2, rows // 2 if low else rows):
            if SWEEPS <= i < keep:
                done = middle[i - SWEEPS, part(g), 0:cols]
            else:
                done = work[SWEEPS % 2, i if low else i - keep, part(g), 0:cols]
            done = done * spread[i, part(g), :]
            for k in range(cols // LANES):
                first = 8 * g * size + k * 8 + i % 8
                result[pl.ds(first, 8, stride=size), :] = done[:, k * LANES : (k + 1) * LANES]
        copies.append(pltpu.make_async_copy(source.at[part(g)], target.at[part(g)], sent.at[g]))
        copies[-1].start()
    for copy in copies:
        copy.wait()


def per_device(
    obs_innovation,
    obs_precision,
    obs_offsets,
    obs_cell,
    obs_counts,
    land_sea,
    diffusivity,
    background_std,
):
    dests, slots = obs_innovation.shape[2:]
    channels, rows, cols = background_std.shape
    width = cols + LANES
    count_rows, count_cols = lax.axis_size("row"), lax.axis_size("col")
    records = dests * slots

    by_slot = lambda x: x.reshape(dests, slots).T
    offsets = obs_offsets.reshape(dests, 2, slots).transpose(1, 2, 0)
    vmem = lambda *shape: pltpu.VMEM(shape, jnp.float32)
    bf16 = lambda *shape: pltpu.VMEM(shape, jnp.bfloat16)
    packed = kernel_call(
        pack_body,
        "pack_records",
        f32(dests, 1, 3 * LANES),
        (by_slot(obs_innovation), by_slot(obs_precision), offsets, by_slot(obs_cell), obs_counts.reshape(1, dests)),
        [
            vmem(slots, dests),
            vmem(slots, dests),
            vmem(2, slots, dests),
            pltpu.VMEM((slots, dests), jnp.int32),
            pltpu.VMEM((1, dests), jnp.int32),
            vmem(LANES, LANES),
            vmem(LANES, LANES),
            pltpu.SemaphoreType.DMA((5,)),
        ],
        moved=200_000,
        place=pltpu.HBM,
        grant=ALL_VMEM_BYTES,
    )
    arrived = lax.all_to_all(packed, "col", split_axis=0, concat_axis=0, tiled=True, axis_index_groups=[list(range(dests))[::-1]])

    spread, coef, far, near = kernel_call(
        fixed_body,
        "fixed_fields",
        (f32(rows, channels, cols), f32(rows, cols), f32(channels + 8, LANES), f32(channels + 8, LANES)),
        (background_std, land_sea, diffusivity),
        [vmem(cols // LANES, channels * rows, LANES)],
        moved=2_000_000,
    )
    far = lax.ppermute(far, "col", [(i, (((i + 1) ^ 1) - 1) % count_cols) for i in range(count_cols)])
    near = lax.ppermute(near, "col", [(i, i ^ 1) for i in range(count_cols)])

    blocks = records // LANES
    chunks = min(CHUNKS, blocks)
    piece = records // chunks
    state, sides = kernel_call(
        build_body,
        "build_state",
        (f32(rows, channels, cols), f32(2, channels, LANES)),
        (arrived, spread),
        [pltpu.VMEM((3, 3, blocks, LANES), jnp.int32), vmem(3, 10, blocks, LANES), vmem(rows * channels, cols)]
        + [bf16(rows * channels, piece)] * (2 * chunks)
        + [bf16(cols, piece)] * (2 * chunks)
        + [bf16(2, 2 * channels, piece)] * chunks
        + [bf16(2, rows * RIM, piece)] * (2 * chunks),
        moved=10_000_000,
    )
    slab = SWEEPS * channels + channels // 2 + 8
    tails, coef_wide, to_up, to_down = kernel_call(
        rim_body,
        "build_rims",
        (f32(rows, channels, LANES), f32(rows, width), f32(slab, cols), f32(slab, cols)),
        (state, sides, coef, far, near),
        moved=2_000_000,
    )
    up = [(i, i + 1) for i in range(count_rows - 1)]
    down = [(j, i) for i, j in up]
    from_down = lax.ppermute(to_up, "row", up)
    from_up = lax.ppermute(to_down, "row", down)

    edge_low, edge_high, middle = kernel_call(
        inner_body,
        "inner_sweeps",
        (
            f32(SWEEPS, 2, channels, width),
            f32(SWEEPS, 2, channels, width),
            f32(rows - 2 * SWEEPS, channels, width),
        ),
        (state, tails, coef_wide),
        [vmem(2, rows, channels, width), vmem(5, rows, width)],
        moved=6_000_000,
    )
    size = rows * cols // LANES
    out = None
    for low, edge, block in ((True, edge_low, from_down), (False, edge_high, from_up)):
        out = kernel_call(
            functools.partial(side_body, low),
            "low_sweeps" if low else "high_sweeps",
            f32(channels, size, LANES),
            (edge, middle, coef_wide, spread, block) + (() if low else (out,)),
            [
                vmem(2, SWEEPS, channels, width),
                vmem(5, rows, width),
                vmem(rows, width),
                vmem(channels * size // 2, LANES),
                pltpu.SemaphoreType.DMA((channels // 8,)),
            ],
            moved=5_000_000,
            held=() if low else (5,),
            out_place=pltpu.HBM,
        )
    out = out.reshape(channels, rows // 8, cols // LANES, 8, LANES)
    return out.transpose(0, 1, 3, 2, 4).reshape(channels, rows, cols)


def solution(mesh):
    placed = (
        P("row", "col", None, None),
        P("row", "col", None, None),
        P("row", "col", None, None, None),
        P("row", "col", None, None),
        P("row", "col", None),
        P("row", "col"),
        P("row", "col"),
        P(None, "row", "col"),
    )
    return jax.shard_map(
        per_device, mesh=mesh, in_specs=placed, out_specs=P(None, "row", "col"), check_vma=False
    )
```

```python
import functools

import jax
import jax.numpy as jnp
from jax import lax
from jax.experimental import pallas as pl
from jax.experimental.pallas import tpu as pltpu
from jax.sharding import PartitionSpec as P

SWEEPS = 6
LANES = 128
CHUNKS = 4
RIM = 8
VMEM_BYTES = 24 * 1024 * 1024
ALL_VMEM_BYTES = 58 * 1024 * 1024

NT = (((1,), (1,)), ((), ()))


def kernel_call(body, name, outs, inputs, scratch=(), moved=0, place=pltpu.VMEM, grant=VMEM_BYTES, held=(), out_place=pltpu.VMEM):
    specs = [pl.BlockSpec(memory_space=out_place if k in held else place) for k in range(len(inputs))]
    return pl.pallas_call(
        body,
        name=name,
        out_shape=outs,
        in_specs=specs,
        out_specs=jax.tree.map(lambda _: pl.BlockSpec(memory_space=out_place), outs),
        scratch_shapes=list(scratch),
        input_output_aliases={k: 0 for k in held},
        compiler_params=pltpu.CompilerParams(vmem_limit_bytes=grant),
        cost_estimate=pl.CostEstimate(flops=0, bytes_accessed=moved, transcendentals=0),
    )(*inputs)


def f32(*shape):
    return jax.ShapeDtypeStruct(shape, jnp.float32)


def pack_body(innovation_in, precision_in, offsets_in, cells_in, counts_in, out, innovation, precision, offsets, cells, counts, tile, rows, arrived, staged, sent):
    pairs = (
        (counts_in, counts),
        (innovation_in, innovation),
        (precision_in, precision),
        (offsets_in, offsets),
        (cells_in, cells),
    )
    copies = [pltpu.make_async_copy(source, held, arrived.at[k]) for k, (source, held) in enumerate(pairs)]
    for copy in copies:
        copy.start()
    for copy in copies:
        copy.wait()
    slots, dests = innovation.shape
    live = lax.broadcasted_iota(jnp.int32, (slots, dests), 0) < counts[...]
    tile[0:slots, 0:dests] = jnp.where(live, innovation[...] * precision[...], 0.0)
    tile[slots : 2 * slots, 0:dests] = offsets[0]
    tile[2 * slots : 3 * slots, 0:dests] = offsets[1]
    tile[3 * slots : 4 * slots, 0:dests] = cells[...].astype(jnp.float32)
    rows[...] = tile[...].T
    half = dests // 2
    leaving = []
    for part in range(2):
        here = slice(part * half, (part + 1) * half)
        for q in range(part * half, (part + 1) * half):
            for k in range(3):
                staged[q, :, k * LANES : (k + 1) * LANES] = rows[pl.ds((dests - 2 - q + k) % dests, 1), :]
        leaving.append(pltpu.make_async_copy(staged.at[here], out.at[here], sent.at[part]))
        leaving[-1].start()
    for copy in leaving:
        copy.wait()


def odd_column():
    return lax.rem(lax.axis_index("col"), 2) == 1


def fixed_body(std, sea, diffusivity, spread, coef, far, near, stage):
    channels, rows, cols = std.shape
    mask = sea[...].astype(jnp.float32)
    product = std[...].astype(jnp.float32) * mask[None]
    for part in range(cols // LANES):
        stage[part] = product[:, :, part * LANES : (part + 1) * LANES].reshape(channels * rows, LANES)
    coef[...] = diffusivity[...] * mask
    lane = lax.broadcasted_iota(jnp.int32, (channels, LANES), 1)
    ends = [jnp.zeros((channels, LANES), jnp.float32)] * 2
    for i in range(rows):
        here = [stage[part, pl.ds(i, channels, stride=rows), :] for part in range(cols // LANES)]
        for part, values in enumerate(here):
            spread[i, :, part * LANES : (part + 1) * LANES] = values
        inside = (lane >= RIM * i) & (lane < RIM * (i + 1))
        ends[0] = jnp.where(inside, pltpu.roll(here[0], (RIM * i) % LANES, 1), ends[0])
        ends[1] = jnp.where(inside, pltpu.roll(here[-1], (RIM * i + RIM) % LANES, 1), ends[1])
    lane_row = lax.broadcasted_iota(jnp.int32, (1, LANES), 1)
    for which in range(2):
        edge = coef[:, 0:LANES] if which == 0 else coef[:, cols - LANES : cols]
        packed = jnp.zeros((1, LANES), jnp.float32)
        for i in range(rows):
            inside = (lane_row >= RIM * i) & (lane_row < RIM * (i + 1))
            turned = pltpu.roll(edge[i : i + 1], (RIM * i + RIM * which) % LANES, 1)
            packed = jnp.where(inside, turned, packed)
        ends[which] = jnp.concatenate([ends[which], jnp.broadcast_to(packed, (8, LANES))], axis=0)
    odd = odd_column()
    near[...] = jnp.where(odd, ends[0], ends[1])
    far[...] = jnp.where(odd, ends[1], ends[0])


def record_fields(block, slots):
    quarter = block.shape[0] // 4
    lane = lax.broadcasted_iota(jnp.int32, (quarter, LANES), 1)
    fields = []
    for f in range(4):
        joined = None
        for b in range(4):
            part = block[b * quarter : (b + 1) * quarter]
            turn = (slots * (b - f)) % LANES
            if turn:
                part = pltpu.roll(part, turn, 1)
            joined = part if b == 0 else jnp.where(lane >= slots * b, part, joined)
        fields.append(joined)
    return fields


def build_body(arrived, spread, state, sides, whole, real, total, *held):
    rows, channels, cols = spread.shape
    slots = LANES // 4
    blocks = whole.shape[2]
    chunks = len(held) // 7
    a_high, a_low, b_high, b_low, c_both, d_high, d_low = [held[q * chunks : (q + 1) * chunks] for q in range(7)]

    for k in range(3):
        weight, east, north, cell = record_fields(arrived[:, 0, k * LANES : (k + 1) * LANES], slots)
        cell = cell.astype(jnp.int32)
        for f, values in enumerate((cell >> 12, (cell >> 8) & 15, cell & 255)):
            whole[k, f] = values
        if k == 1:
            parts = (weight * (1.0 - north), weight * north, 1.0 - east, east)
        else:
            parts = (1.0 - north, north, 1.0 - east, east, weight)
        for f, values in enumerate(parts):
            high = values.astype(jnp.bfloat16).astype(jnp.float32)
            if k == 1 or f == 4:
                real[k, 2 * f] = high
                real[k, 2 * f + 1] = values - high
            else:
                real[k, 2 * f] = values

    def pick(away, at, after):
        return jnp.where(away == 0, at, jnp.where(away == 1, after, 0.0))

    def block(n, c, here):
        row_of = lambda k, f: real[k, f, n : n + 1, :]
        index = lambda k, f, size: lax.broadcasted_iota(jnp.int32, (size, LANES), 0) - whole[k, f, n : n + 1, :]

        hot = jnp.where(index(1, 0, channels) == 0, 1.0, 0.0).astype(jnp.bfloat16)
        away = index(1, 1, rows)
        high, low = pick(away, row_of(1, 0), row_of(1, 2)), pick(away, row_of(1, 1), row_of(1, 3))
        wide = lambda x: jnp.broadcast_to(x, (channels, LANES)).astype(jnp.bfloat16)
        for row in range(rows):
            at = slice(row * channels, (row + 1) * channels)
            a_high[c][at, here] = hot * wide(high[row : row + 1])
            a_low[c][at, here] = hot * wide(low[row : row + 1])
        tile = lambda x: jnp.broadcast_to(x, (16, LANES)).astype(jnp.bfloat16)
        column = whole[1, 2, n : n + 1, :].astype(jnp.float32)
        at, after = tile(column), tile(column + 1.0)
        factors = [tile(row_of(1, f)) for f in (4, 5, 6, 7)]
        none = jnp.zeros((16, LANES), jnp.bfloat16)
        for q in range(cols // 16):
            some = slice(16 * q, 16 * (q + 1))
            line = (lax.broadcasted_iota(jnp.int32, (16, LANES), 0) + 16 * q).astype(jnp.float32).astype(jnp.bfloat16)
            first, second = line == at, line == after
            b_high[c][some, here] = jnp.where(first, factors[0], jnp.where(second, factors[2], none))
            b_low[c][some, here] = jnp.where(first, factors[1], jnp.where(second, factors[3], none))

        for side, (k, base) in enumerate(((0, cols - RIM), (2, 0))):
            hot = index(k, 0, channels) == 0
            for part in range(2):
                at = slice(part * channels, (part + 1) * channels)
                c_both[c][side, at, here] = jnp.where(hot, row_of(k, 8 + part), 0.0).astype(jnp.bfloat16)
            by_row = pick(index(k, 1, rows), row_of(k, 0), row_of(k, 2))
            by_col = pick(index(k, 2, RIM) + base, row_of(k, 4), row_of(k, 6))
            both = (by_row[:, None, :] * by_col[None, :, :]).reshape(rows * RIM, LANES)
            high = both.astype(jnp.bfloat16)
            d_high[c][side, :, here] = high
            d_low[c][side, :, here] = (both - high.astype(jnp.float32)).astype(jnp.bfloat16)

    dot = lambda x, y: lax.dot_general(x, y, NT, preferred_element_type=jnp.float32)
    per = blocks // chunks
    rim = [0.0, 0.0]
    for c in range(chunks):
        for n in range(per):
            block(c * per + n, c, slice(n * LANES, (n + 1) * LANES))
        first, second = b_high[c][...], b_low[c][...]
        part = dot(a_high[c][...], first) + (dot(a_high[c][...], second) + dot(a_low[c][...], first))
        total[...] = part if c == 0 else total[...] + part
        for side in range(2):
            first = dot(c_both[c][side], d_high[c][side])
            second = dot(c_both[c][side, 0:channels], d_low[c][side])
            rim[side] = rim[side] + (first[0:channels] + (first[channels:] + second))
    for side in range(2):
        sides[side] = rim[side]
    for i in range(rows):
        state[i] = total[i * channels : (i + 1) * channels, :] * spread[i]


def rim_body(state, sides, coef, far, near, tails, coef_out, to_up, to_down):
    rows, channels, cols = state.shape
    lane = lax.broadcasted_iota(jnp.int32, (channels, LANES), 1)
    lane_row = lax.broadcasted_iota(jnp.int32, (1, LANES), 1)

    def outer(left, right, i, lanes):
        left = pltpu.roll(left, (LANES - RIM - RIM * i) % LANES, 1)
        right = pltpu.roll(right, (LANES - RIM * i) % LANES, 1)
        return jnp.where(lanes < RIM, right, jnp.where(lanes >= LANES - RIM, left, 0.0))

    odd = odd_column()
    rim_left = jnp.where(odd, near[...], far[...])
    rim_right = jnp.where(odd, far[...], near[...])
    left = sides[0] * rim_left[0:channels]
    right = sides[1] * rim_right[0:channels]
    coef_out[:, 0:cols] = coef[...]
    for i in range(rows):
        tails[i] = outer(left, right, i, lane)
        coef_out[i : i + 1, cols : cols + LANES] = outer(
            rim_left[channels : channels + 1], rim_right[channels : channels + 1], i, lane_row
        )

    for out, start in ((to_down, 0), (to_up, rows - SWEEPS)):
        packed = jnp.zeros((channels, LANES), jnp.float32)
        for q in range(SWEEPS):
            i = start + q
            out[q * channels : (q + 1) * channels, :] = state[i]
            inside = (lane >= 2 * RIM * q) & (lane < 2 * RIM * (q + 1))
            packed = jnp.where(inside, pltpu.roll(tails[i], (2 * RIM * q + RIM) % LANES, 1), packed)
        base = SWEEPS * channels
        half = channels // 2
        out[base : base + half, 0:LANES] = packed[0:half]
        out[base : base + half, LANES : 2 * LANES] = packed[half:channels]
        base = base + half
        out[base : base + 8, :] = jnp.zeros((8, cols), jnp.float32)
        out[base : base + SWEEPS, :] = coef_out[start : start + SWEEPS, 0:cols]
        packed = jnp.zeros((1, LANES), jnp.float32)
        for q in range(SWEEPS):
            inside = (lane_row >= 2 * RIM * q) & (lane_row < 2 * RIM * (q + 1))
            tail = coef_out[start + q : start + q + 1, cols : cols + LANES]
            packed = jnp.where(inside, pltpu.roll(tail, (2 * RIM * q + RIM) % LANES, 1), packed)
        out[base + SWEEPS : base + SWEEPS + 1, 0:LANES] = packed


def set_faces(faces, field):
    rows, width = field.shape
    east = jnp.sqrt(field * pltpu.roll(field, width - 1, 1))
    north = jnp.sqrt(field * pltpu.roll(field, rows - 1, 0))
    west = pltpu.roll(east, 1, 1)
    south = pltpu.roll(north, 1, 0)
    faces[0, 0:rows] = 1.0 - ((east + west) + (north + south))
    for k, values in enumerate((east, west, north, south)):
        faces[1 + k, 0:rows] = values


def turns(load, count, width):
    return [[(pltpu.roll(load(r, g), width - 1, 1), pltpu.roll(load(r, g), 1, 1)) for r in range(count)] for g in range(4)]


def swept(load, turned, faces, first, store):
    width = faces.shape[2]
    for r in range(len(turned[0])):
        c, e, w, n, s = [jnp.broadcast_to(faces[k, pl.ds(first + r, 1), :], (8, width)) for k in range(5)]
        for g in range(len(turned)):
            east, west = turned[g][r]
            store(r, g, (c * load(r, g) + (e * east + w * west)) + (n * load(r + 1, g) + s * load(r - 1, g)))


def side_by_side(state, tails, i, g):
    here = slice(8 * g, 8 * (g + 1))
    return jnp.concatenate([state[i, here, :], tails[i, here, :]], axis=1)


def inner_body(state, tails, coef, edge_low, edge_high, middle, work, faces):
    rows, channels, cols = state.shape
    width = cols + LANES
    part = lambda g: slice(8 * g, 8 * (g + 1))

    set_faces(faces, coef[...])
    for g in range(channels // 8):
        for k in range(2):
            edge_low[0, k, part(g), :] = side_by_side(state, tails, k, g)
            edge_high[0, k, part(g), :] = side_by_side(state, tails, rows - 2 + k, g)

    def loader(t):
        if t == 0:
            return lambda r, g: side_by_side(state, tails, 1 + r, g)
        return lambda r, g: work[t % 2, t + 1 + r, part(g), :]

    def storer(t):
        def store(r, g, values):
            done, row = t + 1, t + 1 + r
            if done == SWEEPS:
                middle[r, part(g), :] = values
                return
            work[done % 2, row, part(g), :] = values
            if row < done + 2:
                edge_low[done, row - done, part(g), :] = values
            if row >= rows - 2 - done:
                edge_high[done, row - (rows - 2 - done), part(g), :] = values

        return store

    for t in range(SWEEPS):
        load, count = loader(t), rows - 2 * (t + 1)
        swept(load, turns(load, count, width), faces, t + 1, storer(t))


def side_body(low, edge, middle, coef, spread, block, *rest):
    out, work, faces, stage, result, sent = rest[-6:]
    rows, channels, cols = spread.shape
    width = cols + LANES
    half = channels // 2
    keep = rows - SWEEPS
    lane = lax.broadcasted_iota(jnp.int32, (channels, LANES), 1)
    part = lambda g: slice(8 * g, 8 * (g + 1))

    base = SWEEPS * channels
    packed = jnp.concatenate([block[base : base + half, 0:LANES], block[base : base + half, LANES : 2 * LANES]], axis=0)
    for q in range(SWEEPS):
        work[0, q, :, 0:cols] = block[q * channels : (q + 1) * channels, :]
        tail = pltpu.roll(packed, (LANES - 2 * RIM * q - RIM) % LANES, 1)
        work[0, q, :, cols:width] = jnp.where((lane < RIM) | (lane >= LANES - RIM), tail, 0.0)
    base = base + half
    start = 0 if low else keep
    stage[start : start + SWEEPS, 0:cols] = block[base : base + SWEEPS, :]
    packed = block[base + SWEEPS : base + SWEEPS + 1, 0:LANES]
    for q in range(SWEEPS):
        tail = pltpu.roll(packed, (LANES - 2 * RIM * q - RIM) % LANES, 1)
        stage[start + q : start + q + 1, cols:width] = jnp.where((lane[0:1] < RIM) | (lane[0:1] >= LANES - RIM), tail, 0.0)
    if low:
        stage[SWEEPS:rows, :] = coef[0:keep, :]
    else:
        stage[0:keep, :] = coef[SWEEPS:rows, :]
    set_faces(faces, stage[...])

    def loader(t):
        def load(r, g):
            j = r + 1 if low else r - 1
            if 0 <= j < SWEEPS:
                return work[t % 2, j, part(g), :]
            return edge[t, j - SWEEPS if low else r + 1, part(g), :]

        return load

    def storer(t):
        def store(r, g, values):
            work[(t + 1) % 2, r, part(g), :] = values

        return store

    for t in range(SWEEPS):
        load = loader(t)
        swept(load, turns(load, SWEEPS, width), faces, t + 1 if low else keep - 1 - t, storer(t))

    size = rows // 2 * cols // LANES
    target = out.at[:, 0:size, :] if low else out.at[:, size : 2 * size, :]
    source = result.reshape(channels, size, LANES)
    copies = []
    for g in range(channels // 8):
        for i in range(0 if low else rows // 2, rows // 2 if low else rows):
            if SWEEPS <= i < keep:
                done = middle[i - SWEEPS, part(g), 0:cols]
            else:
                done = work[SWEEPS % 2, i if low else i - keep, part(g), 0:cols]
            done = done * spread[i, part(g), :]
            for k in range(cols // LANES):
                first = 8 * g * size + k * 8 + i % 8
                result[pl.ds(first, 8, stride=size), :] = done[:, k * LANES : (k + 1) * LANES]
        copies.append(pltpu.make_async_copy(source.at[part(g)], target.at[part(g)], sent.at[g]))
        copies[-1].start()
    for copy in copies:
        copy.wait()


def per_device(
    obs_innovation,
    obs_precision,
    obs_offsets,
    obs_cell,
    obs_counts,
    land_sea,
    diffusivity,
    background_std,
):
    dests, slots = obs_innovation.shape[2:]
    channels, rows, cols = background_std.shape
    width = cols + LANES
    count_rows, count_cols = lax.axis_size("row"), lax.axis_size("col")
    records = dests * slots

    by_slot = lambda x: x.reshape(dests, slots).T
    offsets = obs_offsets.reshape(dests, 2, slots).transpose(1, 2, 0)
    vmem = lambda *shape: pltpu.VMEM(shape, jnp.float32)
    bf16 = lambda *shape: pltpu.VMEM(shape, jnp.bfloat16)
    packed = kernel_call(
        pack_body,
        "pack_records",
        f32(dests, 1, 3 * LANES),
        (by_slot(obs_innovation), by_slot(obs_precision), offsets, by_slot(obs_cell), obs_counts.reshape(1, dests)),
        [
            vmem(slots, dests),
            vmem(slots, dests),
            vmem(2, slots, dests),
            pltpu.VMEM((slots, dests), jnp.int32),
            pltpu.VMEM((1, dests), jnp.int32),
            vmem(LANES, LANES),
            vmem(LANES, LANES),
            pltpu.SemaphoreType.DMA((5,)),
            vmem(dests, 1, 3 * LANES),
            pltpu.SemaphoreType.DMA((2,)),
        ],
        moved=200_000,
        place=pltpu.HBM,
        grant=ALL_VMEM_BYTES,
        out_place=pltpu.HBM,
    )
    arrived = lax.all_to_all(packed, "col", split_axis=0, concat_axis=0, tiled=True, axis_index_groups=[list(range(dests))[::-1]])

    spread, coef, far, near = kernel_call(
        fixed_body,
        "fixed_fields",
        (f32(rows, channels, cols), f32(rows, cols), f32(channels + 8, LANES), f32(channels + 8, LANES)),
        (background_std, land_sea, diffusivity),
        [vmem(cols // LANES, channels * rows, LANES)],
        moved=2_000_000,
    )
    far = lax.ppermute(far, "col", [(i, (((i + 1) ^ 1) - 1) % count_cols) for i in range(count_cols)])
    near = lax.ppermute(near, "col", [(i, i ^ 1) for i in range(count_cols)])

    blocks = records // LANES
    chunks = min(CHUNKS, blocks)
    piece = records // chunks
    state, sides = kernel_call(
        build_body,
        "build_state",
        (f32(rows, channels, cols), f32(2, channels, LANES)),
        (arrived, spread),
        [pltpu.VMEM((3, 3, blocks, LANES), jnp.int32), vmem(3, 10, blocks, LANES), vmem(rows * channels, cols)]
        + [bf16(rows * channels, piece)] * (2 * chunks)
        + [bf16(cols, piece)] * (2 * chunks)
        + [bf16(2, 2 * channels, piece)] * chunks
        + [bf16(2, rows * RIM, piece)] * (2 * chunks),
        moved=10_000_000,
    )
    slab = SWEEPS * channels + channels // 2 + 8
    tails, coef_wide, to_up, to_down = kernel_call(
        rim_body,
        "build_rims",
        (f32(rows, channels, LANES), f32(rows, width), f32(slab, cols), f32(slab, cols)),
        (state, sides, coef, far, near),
        moved=2_000_000,
    )
    up = [(i, i + 1) for i in range(count_rows - 1)]
    down = [(j, i) for i, j in up]
    from_down = lax.ppermute(to_up, "row", up)
    from_up = lax.ppermute(to_down, "row", down)

    edge_low, edge_high, middle = kernel_call(
        inner_body,
        "inner_sweeps",
        (
            f32(SWEEPS, 2, channels, width),
            f32(SWEEPS, 2, channels, width),
            f32(rows - 2 * SWEEPS, channels, width),
        ),
        (state, tails, coef_wide),
        [vmem(2, rows, channels, width), vmem(5, rows, width)],
        moved=6_000_000,
    )
    size = rows * cols // LANES
    out = None
    for low, edge, block in ((True, edge_low, from_down), (False, edge_high, from_up)):
        out = kernel_call(
            functools.partial(side_body, low),
            "low_sweeps" if low else "high_sweeps",
            f32(channels, size, LANES),
            (edge, middle, coef_wide, spread, block) + (() if low else (out,)),
            [
                vmem(2, SWEEPS, channels, width),
                vmem(5, rows, width),
                vmem(rows, width),
                vmem(channels * size // 2, LANES),
                pltpu.SemaphoreType.DMA((channels // 8,)),
            ],
            moved=5_000_000,
            held=() if low else (5,),
            out_place=pltpu.HBM,
        )
    out = out.reshape(channels, rows // 8, cols // LANES, 8, LANES)
    return out.transpose(0, 1, 3, 2, 4).reshape(channels, rows, cols)


def solution(mesh):
    placed = (
        P("row", "col", None, None),
        P("row", "col", None, None),
        P("row", "col", None, None, None),
        P("row", "col", None, None),
        P("row", "col", None),
        P("row", "col"),
        P("row", "col"),
        P(None, "row", "col"),
    )
    return jax.shard_map(
        per_device, mesh=mesh, in_specs=placed, out_specs=P(None, "row", "col"), check_vma=False
    )
```
